256 devices in a mesh: wide: 64 (over z, x, core), narrow: 4 (over y).
Axes of the slice: x: 4, y: 4, z: 8, core: 2. Of those that a mesh axis runs over, the one named last changes fastest.
Arguments:
- snapshots: bfloat16 [524288, 512], P('wide', 'narrow'), may hold values from -16 to 16
Outputs:
- basis: float32 [524288, 128], P('wide', 'narrow')
- energies: float32 [128], P('narrow')
The draws below stay inside these ranges and needn't reach their ends.
All inputs are finite; a program needn't handle non-finite values.
Results may differ from the reference program's by a relative error of at most 0.012.
Values may be sent and summed in bfloat16 or wider, within the bound.
A program may use at most 64 MiB of HBM per device.

```python
import math
import jax
import jax.numpy as jnp
from jax import lax

R = 128
ITERS = 3
P_SIZE = 524288
SNAP = 512
N_NARROW = 4


def draw_snapshots(key, part):
    key = jax.random.fold_in(key, 11)
    key_noise, key_scale, key_modes, key_coefs = jax.random.split(key, 4)
    noise = jax.random.normal(key_noise, (P_SIZE, SNAP), jnp.float32)
    spread = math.log(4.0)
    weight = 0.25
    row_low = 0.4
    row_ratio = 5.0
    column_scale = jnp.exp(jax.random.uniform(key_scale, (SNAP,), jnp.float32, 0.0, spread))
    modes = jax.random.normal(key_modes, (P_SIZE, 4), jnp.float32)
    coefs = jax.random.normal(key_coefs, (4, SNAP), jnp.float32) * weight
    values = noise * column_scale[None, :]
    for index in range(4):
        values = values + modes[:, index:index + 1] * coefs[index:index + 1, :]
    position = jnp.arange(P_SIZE, dtype=jnp.float32) / jnp.float32(P_SIZE)
    row_scale = jnp.float32(row_low) * jnp.exp(position * jnp.float32(math.log(row_ratio)))
    values = values * row_scale[:, None]
    return jnp.clip(values, -16.0, 16.0).astype(jnp.bfloat16)


def setup_inputs(seed: int = 0) -> dict:
    splits = jax.random.split(jax.random.key(seed), 2)
    return {
        "snapshots": draw_snapshots(jax.random.fold_in(splits[1], 71), 0),
    }


epsilon = 1e-06

def orthonormal(tall):
    inner = jnp.dot(tall.T.astype(jnp.float32), tall.astype(jnp.float32), precision=lax.Precision.HIGHEST, preferred_element_type=jnp.float32)
    lower_factor = jnp.linalg.cholesky(inner)
    return lax.linalg.triangular_solve(lower_factor, tall, left_side=False, lower=True, transpose_a=True)

def rotation(gram_sum, basis_width):
    identity_block = jnp.eye(basis_width, dtype=jnp.float32)
    current = jnp.concatenate([identity_block, identity_block], axis=0) * jnp.float32(0.5 ** 0.5)
    for sweep in range(ITERS):
        current = orthonormal(jnp.dot(gram_sum.astype(jnp.float32), current.astype(jnp.float32), precision=lax.Precision.HIGHEST, preferred_element_type=jnp.float32))
    return current.astype(jnp.bfloat16)

def merge_pair(lower_block, upper_block):
    paired = jnp.concatenate([lower_block, upper_block], axis=1)
    paired_wide = paired.astype(jnp.float32)
    gram_sum = jnp.dot(paired_wide.T.astype(jnp.float32), paired_wide.astype(jnp.float32), precision=lax.Precision.HIGHEST, preferred_element_type=jnp.float32)
    factor = rotation(gram_sum, lower_block.shape[1])
    return jnp.dot(paired.astype(jnp.float32), factor.astype(jnp.float32), preferred_element_type=jnp.float32)

def reference(snapshots):
    blocks = [snapshots[:, index * R:(index + 1) * R] for index in range(N_NARROW)]
    while len(blocks) > 1:
        merged_list = []
        for index in range(len(blocks) // 2):
            merged = merge_pair(blocks[2 * index], blocks[2 * index + 1])
            if len(blocks) > 2:
                merged = merged.astype(jnp.bfloat16)
            merged_list.append(merged)
        blocks = merged_list
    final_block = blocks[0]
    energies = jnp.sqrt(lax.optimization_barrier(jnp.sum(final_block * final_block, axis=0)) + epsilon)
    return (final_block / energies, energies)
```

```python
import functools
import jax
import jax.numpy as jnp
from jax import lax
from jax.experimental import pallas as pl
from jax.experimental.pallas import tpu as pltpu
from jax.sharding import PartitionSpec as P

MESH = pl.DeviceIdType.MESH
F32 = jnp.float32
PAIRS = ((0, 0), (0, 1), (1, 1), (2, 2), (2, 3), (3, 3), (0, 2), (0, 3), (1, 2), (1, 3))
PARTS = ((0, 768), (768, 512))
VLIM = 48 * 1024 * 1024


def where_am_i():
    w = lax.axis_index("wide")
    y = lax.axis_index("narrow")
    return lax.rem(w, 2), lax.rem(lax.div(w, 2), 4), y, lax.div(w, 8)


def device(core, x, y, z):
    return {"wide": (z * 4 + x) * 2 + core, "narrow": y}


def greet(peers):
    barrier = pltpu.get_barrier_semaphore()
    for peer in peers:
        pl.semaphore_signal(barrier, inc=1, device_id=peer, device_id_type=MESH)
    pl.semaphore_wait(barrier, len(peers))


def remote(src, dst, send, recv, peer):
    return pltpu.make_async_remote_copy(src_ref=src, dst_ref=dst, send_sem=send, recv_sem=recv,
                                        device_id=peer, device_id_type=MESH)


def at(start, size, align=8):
    return pl.ds(pl.multiple_of(start, align), size)


def rows_kernel(s_ref, rows_ref, g_ref, stage_ref, send, recv, own_sem, *, gram=True, chunks=4, hw=False):
    core, x, y, z = where_am_i()
    R = rows_ref.shape[1]
    n = R // chunks
    up, down, far = (device(core, x, lax.rem(y + k, 4), z) for k in (1, 3, 2))
    to_up, to_down, to_far = lax.rem(y + 1, 4), lax.rem(y + 3, 4), lax.rem(y + 2, 4)
    greet([up, down, far])
    own = pltpu.make_async_copy(s_ref.at[at(y * R, R, 16)], rows_ref.at[y], own_sem)
    own.start()
    direct = [[], []]
    stage = [[], []]
    forward = [[], []]
    half = chunks // 2
    if not hw:
        for c in range(half):
            for side, peer in ((0, up), (1, down)):
                stage[side].append(remote(
                    s_ref.at[at(to_far * R + (side * half + c) * n, n, 16)], stage_ref.at[side, c],
                    send.at[side, c], recv.at[side, c], peer))
                stage[side][c].start()
    for c in range(chunks):
        for side, peer, row in ((0, up, to_up), (1, down, to_down)):
            direct[side].append(remote(
                s_ref.at[at(row * R + c * n, n, 16)], rows_ref.at[y, pl.ds(c * n, n)],
                send.at[side, half + c], recv.at[side, half + c], peer))
            direct[side][c].start()
    for c in range(half):
        for side, peer, origin in ((0, up, to_down), (1, down, to_up)):
            if hw:
                forward[side].append(remote(
                    s_ref.at[at(to_far * R + (side * half + c) * n, n, 16)],
                    rows_ref.at[y, pl.ds((side * half + c) * n, n)],
                    send.at[side, half + chunks + c], recv.at[side, half + chunks + c], far))
            else:
                stage[side][c].wait_recv()
                forward[side].append(remote(
                    stage_ref.at[side, c], rows_ref.at[origin, pl.ds((side * half + c) * n, n)],
                    send.at[side, half + chunks + c], recv.at[side, half + chunks + c], peer))
            forward[side][c].start()
    own.wait()
    if gram:
        g_ref[...] = jnp.zeros_like(g_ref)
    order = [c for pair in zip(range(half), range(half, chunks)) for c in pair]
    for c in order:
        direct[0][c].wait_recv()
        direct[1][c].wait_recv()
        forward[c // half][c % half].wait_recv()
        if gram:
            blocks = [rows_ref[j, pl.ds(c * n, n), :] for j in range(4)]
            for i in range(4):
                right = jnp.concatenate(blocks[i:], axis=1)
                part = lax.dot_general(blocks[i], right, (((0,), (0,)), ((), ())), preferred_element_type=F32)
                for j in range(i, 4):
                    b = PAIRS.index((i, j))
                    g_ref[128 * b:128 * b + 128, :] += part[:, 128 * (j - i):128 * (j - i) + 128]
    for side in (0, 1):
        for copy in stage[side] + direct[side] + forward[side]:
            copy.wait_send()


def rows(s, gram=True, chunks=4, hw=False, cid=0):
    R = s.shape[0] // 4
    return pl.pallas_call(
        functools.partial(rows_kernel, gram=gram, chunks=chunks, hw=hw),
        out_shape=(jax.ShapeDtypeStruct((4, R, 128), jnp.bfloat16), jax.ShapeDtypeStruct((1280, 128), F32)),
        in_specs=[pl.BlockSpec(memory_space=pl.ANY)],
        out_specs=(pl.BlockSpec(memory_space=pltpu.VMEM),) * 2,
        scratch_shapes=[
            pltpu.VMEM((2, chunks // 2, R // chunks, 128), jnp.bfloat16),
            pltpu.SemaphoreType.DMA((2, 2 * chunks)),
            pltpu.SemaphoreType.DMA((2, 2 * chunks)),
            pltpu.SemaphoreType.DMA,
        ],
        compiler_params=pltpu.CompilerParams(collective_id=cid, has_side_effects=True, vmem_limit_bytes=VLIM),
    )(s)


def sum_kernel(g_ref, out_ref, from_core, halves, from_plane, column, send, recv, *, parts=PARTS):
    core, x, y, z = where_am_i()
    sibling = device(1 - core, x, y, z)
    plane = [(d, lax.rem(x + d // 4, 4), lax.rem(y + d % 4, 4)) for d in range(1, 16)]
    line = [(d, lax.rem(z + d, 8)) for d in range(1, 8)]
    greet([sibling] + [device(core, px, py, z) for _, px, py in plane] + [device(core, x, y, pz) for _, pz in line])
    q = x * 4 + y

    def sizes(p):
        start, rows_ = parts[p]
        half = rows_ // 2
        return start, half, half // 16, start // 2

    each = range(len(parts))
    swap = []
    for p in each:
        start, half, piece, hs = sizes(p)
        swap.append(remote(g_ref.at[at(start + (1 - core) * half, half)], from_core.at[pl.ds(hs, half)],
                           send.at[p, 0, 0], recv.at[p, 0, 0], sibling))
        swap[p].start()
    spread = []
    for p in each:
        start, half, piece, hs = sizes(p)
        swap[p].wait_recv()
        halves[pl.ds(hs, half), :] = g_ref[at(start + core * half, half), :] + from_core[pl.ds(hs, half), :]
        spread.append([remote(halves.at[at(hs + (px * 4 + py) * piece, piece)], from_plane.at[d, pl.ds(hs // 16, piece)],
                              send.at[p, 1, d], recv.at[p, 1, d], device(core, px, py, z)) for d, px, py in plane])
        for copy in spread[p]:
            copy.start()
    ring = []
    for p in each:
        start, half, piece, hs = sizes(p)
        total = halves[at(hs + q * piece, piece), :]
        for (d, _, _), copy in zip(plane, spread[p]):
            copy.wait_recv()
            total = total + from_plane[d, pl.ds(hs // 16, piece), :]
        column[z, pl.ds(hs // 16, piece), :] = total
        mine = column.at[z, pl.ds(hs // 16, piece)]
        ring.append([remote(mine, mine, send.at[p, 2, d], recv.at[p, 2, d], device(core, x, y, pz)) for d, pz in line])
        for copy in ring[p]:
            copy.start()
    back = []
    for p in each:
        start, half, piece, hs = sizes(p)
        for copy in ring[p]:
            copy.wait_recv()
        total = column[0, pl.ds(hs // 16, piece), :]
        for k in range(1, 8):
            total = total + column[k, pl.ds(hs // 16, piece), :]
        own = at(start + core * half + q * piece, piece)
        out_ref[own, :] = total
        back.append([remote(out_ref.at[own], out_ref.at[own], send.at[p, 3, d], recv.at[p, 3, d], device(core, px, py, z))
                     for d, px, py in plane])
        for copy in back[p]:
            copy.start()
    last = []
    for p in each:
        start, half, piece, hs = sizes(p)
        for copy in back[p]:
            copy.wait_recv()
        mine = out_ref.at[at(start + core * half, half)]
        last.append(remote(mine, mine, send.at[p, 4, 0], recv.at[p, 4, 0], sibling))
        last[p].start()
    for p in each:
        last[p].wait_recv()
        for copy in [swap[p], last[p]] + spread[p] + ring[p] + back[p]:
            copy.wait_send()


def allsum(g, cid=1, parts=PARTS):
    rows_ = sum(n for _, n in parts)
    return pl.pallas_call(
        functools.partial(sum_kernel, parts=parts),
        out_shape=jax.ShapeDtypeStruct((rows_, 128), F32),
        in_specs=[pl.BlockSpec(memory_space=pltpu.VMEM)],
        out_specs=pl.BlockSpec(memory_space=pltpu.VMEM),
        scratch_shapes=[
            pltpu.VMEM((rows_ // 2, 128), F32),
            pltpu.VMEM((rows_ // 2, 128), F32),
            pltpu.VMEM((16, rows_ // 32, 128), F32),
            pltpu.VMEM((8, rows_ // 32, 128), F32),
            pltpu.SemaphoreType.DMA((len(parts), 5, 16)),
            pltpu.SemaphoreType.DMA((len(parts), 5, 16)),
        ],
        compiler_params=pltpu.CompilerParams(collective_id=cid, has_side_effects=True, vmem_limit_bytes=VLIM),
    )(g)


def out_kernel(rows_ref, w_ref, e_ref, basis_ref, energy_ref, sent, got, send, recv, *, chunks=4):
    core, x, y, z = where_am_i()
    R = rows_ref.shape[1]
    n = R // chunks
    peers = [(k, lax.rem(y + k, 4)) for k in (2, 1, 3)]
    greet([device(core, x, py, z) for _, py in peers])
    copies = []
    for c in range(chunks):
        block = jnp.concatenate([rows_ref[j, pl.ds(c * n, n), :] for j in range(4)], axis=1)
        part = lax.dot_general(w_ref[...], block, (((0,), (1,)), ((), ())), preferred_element_type=F32)
        part = part.astype(jnp.bfloat16)
        for j in range(4):
            sent[j, :, pl.ds(c * n, n)] = part[32 * j:32 * j + 32, :]
        for k, py in peers:
            copies.append(remote(sent.at[py, :, pl.ds(c * n, n)], got.at[y, :, pl.ds(c * n, n)],
                                 send.at[k, c], recv.at[k, c], device(core, x, py, z)))
            copies[-1].start()
    basis_ref[:, at(y * R, R, 128)] = sent[y].astype(F32)
    energy = jnp.zeros((1, 32), F32)
    for j in range(4):
        energy = jnp.where(y == j, e_ref[0:1, 32 * j:32 * j + 32], energy)
    energy_ref[...] = energy
    for copy in copies:
        copy.wait_recv()
    for k, _ in peers:
        source = lax.rem(y + 4 - k, 4)
        basis_ref[:, at(source * R, R, 128)] = got[source].astype(F32)
    for copy in copies:
        copy.wait_send()


def output(rows_, w, e, cid=2, chunks=4):
    R = rows_.shape[1]
    return pl.pallas_call(
        functools.partial(out_kernel, chunks=chunks),
        out_shape=(jax.ShapeDtypeStruct((32, 4 * R), F32), jax.ShapeDtypeStruct((1, 32), F32)),
        in_specs=[pl.BlockSpec(memory_space=pltpu.VMEM)] * 3,
        out_specs=(pl.BlockSpec(memory_space=pltpu.VMEM),) * 2,
        scratch_shapes=[
            pltpu.VMEM((4, 32, R), jnp.bfloat16),
            pltpu.VMEM((4, 32, R), jnp.bfloat16),
            pltpu.SemaphoreType.DMA((4, chunks)),
            pltpu.SemaphoreType.DMA((4, chunks)),
        ],
        compiler_params=pltpu.CompilerParams(collective_id=cid, has_side_effects=True, vmem_limit_bytes=VLIM),
    )(rows_, w, e)


HI = lax.Precision.HIGHEST


def dot(a, b, ca, cb, precision=HI):
    return lax.dot_general(a, b, (((ca,), (cb,)), ((), ())), precision=precision,
                           preferred_element_type=F32)


def inverse_cholesky(mats, outer=4):
    n = 128
    lane = lax.broadcasted_iota(jnp.int32, (8, n), 1)
    sub = lax.broadcasted_iota(jnp.int32, (8, n), 0)
    S = [[a[8 * r:8 * r + 8, :] for r in range(n // 8)] for a in mats]
    M = range(len(mats))
    panels = n // 8 // outer
    for panel in range(panels):
        first, last = outer * panel, outer * (panel + 1)
        for p in range(first, last):
            base = 8 * p
            inblock = (lane >= base) & (lane < base + 8)
            E = [[[jnp.broadcast_to(S[m][r][:, base + j:base + j + 1], (8, n)) for r in range(p, last)]
                  for j in range(8)] for m in M]
            for m in M:
                for r in range(p, last):
                    fill = jnp.where(lane - base == sub, 1.0, 0.0) if r == p else 0.0
                    S[m][r] = jnp.where(inblock, fill, S[m][r])
            scale = [jnp.zeros((8, n), F32) for m in M]
            for k in range(8):
                inv = [1.0 / jnp.broadcast_to(E[m][k][0][k:k + 1, :], (8, n)) for m in M]
                for m in M:
                    scale[m] = jnp.where(sub == k, inv[m], scale[m])
                    rows = [jnp.broadcast_to(E[m][j][0][k:k + 1, :], (8, n)) for j in range(k + 1, 8)]
                    pivot_row = jnp.broadcast_to(S[m][p][k:k + 1, :], (8, n))
                    for i, r in enumerate(range(p, last)):
                        mult = E[m][k][i] * inv[m]
                        if r == p:
                            mult = jnp.where(sub > k, mult, 0.0)
                        for j in range(k + 1, 8):
                            E[m][j][i] = E[m][j][i] - mult * rows[j - k - 1]
                        S[m][r] = S[m][r] - mult * pivot_row
            for m in M:
                S[m][p] = S[m][p] * jnp.sqrt(scale[m])
        if last < n // 8:
            for m in M:
                left = jnp.concatenate([jnp.where(lane >= 8 * last, S[m][p], 0.0) for p in range(first, last)], axis=0)
                right = jnp.concatenate(
                    [jnp.where((lane >= 8 * last) | (lane < 8 * p + 8), S[m][p], 0.0) for p in range(first, last)], axis=0)
                update = dot(left, right, 0, 0)
                outside = (lane < 8 * first) | (lane >= 8 * last)
                for r in range(last, n // 8):
                    S[m][r] = jnp.where(outside, S[m][r], 0.0) - update[8 * r:8 * r + 8, :]
    out = []
    for m in M:
        out.append(jnp.concatenate(
            [jnp.where(lane <= sub + 8 * r, S[m][r], 0.0) for r in range(n // 8)], axis=0))
    return out


def level(g_refs, x_ref, outer=4):
    half = F32(0.5 ** 0.5)
    row = lax.broadcasted_iota(jnp.int32, (256, 128), 0)
    col = lax.broadcasted_iota(jnp.int32, (256, 128), 1)
    start = jnp.where((row == col) | (row == col + 128), half, F32(0.0))
    for m in range(len(g_refs)):
        x_ref[m] = start

    def sweep(_, carry):
        ys = [dot(g[...], x_ref[m], 1, 0) for m, g in enumerate(g_refs)]
        inner = [dot(y, y, 0, 0) for y in ys]
        linv = inverse_cholesky(inner, outer)
        for m, y in enumerate(ys):
            x_ref[m] = dot(y, linv[m], 1, 1)
        return carry

    lax.fori_loop(0, 3, sweep, 0)
    return [x_ref[m].astype(jnp.bfloat16).astype(F32) for m in range(len(g_refs))]


def chain_kernel(blocks_ref, w_ref, e_ref, x_ref, g1_ref, g_ref, outer=4):
    for b, (i, j) in enumerate(PAIRS):
        block = blocks_ref[128 * b:128 * b + 128, :]
        g_ref[128 * i:128 * i + 128, 128 * j:128 * j + 128] = block
        if (i, j) in ((0, 1), (2, 3)):
            g_ref[128 * j:128 * j + 128, 128 * i:128 * i + 128] = block.T
    f0, f1 = level([g_ref.at[0:256, 0:256], g_ref.at[256:512, 256:512]], x_ref, outer)
    b0 = dot(g_ref[0:256, 0:256], f0, 1, 0)
    b01 = dot(g_ref[0:256, 256:512], f1, 1, 0)
    b1 = dot(g_ref[256:512, 256:512], f1, 1, 0)
    c01 = dot(f0, b01, 0, 0)
    g1_ref[0:128, 0:128] = dot(f0, b0, 0, 0)
    g1_ref[0:128, 128:256] = c01
    g1_ref[128:256, 0:128] = c01.T
    g1_ref[128:256, 128:256] = dot(f1, b1, 0, 0)
    f, = level([g1_ref], x_ref, outer)
    squares = jnp.sum(f * dot(g1_ref[...], f, 1, 0), axis=0, keepdims=True)
    energies = jnp.sqrt(squares + 1e-6)
    e_ref[...] = jnp.broadcast_to(energies, (8, 128))
    inv = 1.0 / energies
    w_ref[0:256, :] = (dot(f0, f[0:128], 1, 0) * inv).astype(jnp.bfloat16)
    w_ref[256:512, :] = (dot(f1, f[128:256], 1, 0) * inv).astype(jnp.bfloat16)


def chain(g, outer=4):
    return pl.pallas_call(
        functools.partial(chain_kernel, outer=outer),
        out_shape=(jax.ShapeDtypeStruct((512, 128), jnp.bfloat16), jax.ShapeDtypeStruct((8, 128), F32)),
        in_specs=[pl.BlockSpec(memory_space=pltpu.VMEM)],
        out_specs=(pl.BlockSpec(memory_space=pltpu.VMEM),) * 2,
        scratch_shapes=[pltpu.VMEM((2, 256, 128), F32), pltpu.VMEM((256, 256), F32),
                        pltpu.VMEM((512, 512), F32)],
        compiler_params=pltpu.CompilerParams(vmem_limit_bytes=32 * 1024 * 1024),
    )(g)


def body(snapshots):
    own_rows, gram = rows(snapshots)
    gram = allsum(gram)
    weights, lengths = chain(gram)
    basis, energies = output(own_rows, weights, lengths)
    return basis.T, energies.reshape(32)


def solution(mesh):
    return jax.shard_map(body, mesh=mesh, in_specs=(P("wide", "narrow"),), out_specs=(P("wide", "narrow"), P("narrow")),
                         check_vma=False)
```

```python
import functools

import jax
import jax.numpy as jnp
from jax import lax
from jax.experimental import pallas as pl
from jax.experimental.pallas import tpu as pltpu
from jax.sharding import PartitionSpec as P

MESH = pl.DeviceIdType.MESH
HI = lax.Precision.HIGHEST
F32 = jnp.float32
BF16 = jnp.bfloat16
SWEEPS = 3
EPSILON = 1e-6
BLOCKS = ((0, 0), (0, 1), (1, 1), (2, 2), (2, 3), (3, 3), (0, 2), (0, 3), (1, 2), (1, 3))
PARTS = ((0, 768), (768, 512))
CHUNKS = 4


def dot(a, b, ca, cb, precision=HI):
    return lax.dot_general(a, b, (((ca,), (cb,)), ((), ())), precision=precision, preferred_element_type=F32)


def inverse_cholesky(mats, outer=4, wide=2):
    n = 128
    lane = lax.broadcasted_iota(jnp.int32, (8, n), 1)
    sub = lax.broadcasted_iota(jnp.int32, (8, n), 0)
    S = [[a[8 * r:8 * r + 8, :] for r in range(n // 8)] for a in mats]
    M = range(len(mats))
    full = lambda row: jnp.broadcast_to(row, (8, n))
    for first in range(0, n // 8, outer):
        last = first + outer
        for p in range(first, last, wide):
            base = 8 * p
            inblock = (lane >= base) & (lane < base + 8 * wide)
            E = [[{r: full(S[m][r][:, base + j:base + j + 1]) for r in range(p + j // 8, last)}
                  for j in range(8 * wide)] for m in M]
            for m in M:
                for r in range(p, last):
                    fill = jnp.where(lane - 8 * r == sub, 1.0, 0.0) if r < p + wide else 0.0
                    S[m][r] = jnp.where(inblock, fill, S[m][r])
            scale = [[jnp.zeros((8, n), F32)] * wide for m in M]
            for k in range(8 * wide):
                top, row = p + k // 8, k % 8
                inv = [1.0 / full(E[m][k][top][row:row + 1, :]) for m in M]
                for m in M:
                    scale[m][k // 8] = jnp.where(sub == row, inv[m], scale[m][k // 8])
                    pivots = {j: full(E[m][k][p + j // 8][j % 8:j % 8 + 1, :]) for j in range(k + 1, 8 * wide)}
                    pivot_row = full(S[m][top][row:row + 1, :])
                    for r in range(top, last):
                        mult = E[m][k][r] * inv[m]
                        if r == top:
                            mult = jnp.where(sub > row, mult, 0.0)
                        for j in range(k + 1, 8 * wide):
                            if r >= p + j // 8:
                                E[m][j][r] = E[m][j][r] - mult * pivots[j]
                        S[m][r] = S[m][r] - mult * pivot_row
            for m in M:
                for i in range(wide):
                    S[m][p + i] = S[m][p + i] * jnp.sqrt(scale[m][i])
        if last < n // 8:
            for m in M:
                left = jnp.concatenate([jnp.where(lane >= 8 * last, S[m][p], 0.0) for p in range(first, last)], axis=0)
                right = jnp.concatenate(
                    [jnp.where((lane >= 8 * last) | (lane < 8 * (p - (p - first) % wide + wide)), S[m][p], 0.0)
                     for p in range(first, last)], axis=0)
                update = dot(left, right, 0, 0)
                outside = (lane < 8 * first) | (lane >= 8 * last)
                for r in range(last, n // 8):
                    S[m][r] = jnp.where(outside, S[m][r], 0.0) - update[8 * r:8 * r + 8, :]
    return [jnp.concatenate([jnp.where(lane <= sub + 8 * r, S[m][r], 0.0) for r in range(n // 8)], axis=0) for m in M]


def device(core, x, y, z):
    return {"wide": (z * 4 + x) * 2 + core, "narrow": y}


def remote(src, dst, send, recv, peer):
    return pltpu.make_async_remote_copy(src_ref=src, dst_ref=dst, send_sem=send, recv_sem=recv,
                                        device_id=peer, device_id_type=MESH)


def at(start, size, align=8):
    return pl.ds(pl.multiple_of(start, align), size)


def start_all(copies):
    for copy in copies:
        copy.start()
    return copies


def level(grams, y_ref, between=None):
    for m, g in enumerate(grams):
        y_ref[m] = (g[:, 0:128] + g[:, 128:256]) * F32(0.5 ** 0.5)

    def sweep(step, carry):
        ys = [y_ref[m] for m in range(len(grams))]
        linv = inverse_cholesky([dot(v, v, 0, 0) for v in ys])
        ahead = [jnp.where(step == SWEEPS - 1, v, dot(g[...], v, 1, 0)) for g, v in zip(grams, ys)]
        for m, v in enumerate(ahead):
            y_ref[m] = dot(v, linv[m], 1, 1)
        if between is not None:
            between(step)
        return carry

    lax.fori_loop(0, SWEEPS, sweep, 0)
    return [y_ref[m].astype(BF16).astype(F32) for m in range(len(grams))]


def kernel(s_ref, basis_ref, energy_ref, rows_ref, part_ref, sum_ref, from_core, halves, from_plane, column,
           g_ref, g1_ref, x_ref, sent_ref, got_ref,
           own_sem, row_send, row_recv, sum_send, sum_recv, out_send, out_recv):
    w = lax.axis_index("wide")
    y = lax.axis_index("narrow")
    core, x, z = lax.rem(w, 2), lax.rem(lax.div(w, 2), 4), lax.div(w, 8)
    R = rows_ref.shape[1]
    n = R // CHUNKS
    sibling = device(1 - core, x, y, z)
    plane = [(d, lax.rem(x + d // 4, 4), lax.rem(y + d % 4, 4)) for d in range(1, 16)]
    line = [(d, lax.rem(z + d, 8)) for d in range(1, 8)]

    barrier = pltpu.get_barrier_semaphore()
    peers = [device(core, x, y, pz) for d, pz in sorted(line, key=lambda v: abs(v[0] - 4))]
    peers += [device(core, px, py, z) for d, px, py in sorted(plane, key=lambda v: abs(v[0] // 4 - 2) + abs(v[0] % 4 - 2))]
    peers += [sibling]
    for peer in peers:
        pl.semaphore_signal(barrier, inc=1, device_id=peer, device_id_type=MESH)
    own = pltpu.make_async_copy(s_ref.at[at(y * R, R, 16)], rows_ref.at[y], own_sem)
    own.start()
    part_ref[...] = jnp.zeros_like(part_ref)
    pl.semaphore_wait(barrier, len(peers))

    moves = []
    for c in range(CHUNKS):
        moves.append([])
        for k in (2, 1, 3):
            py = lax.rem(y + k, 4)
            moves[c].append(remote(s_ref.at[at(py * R + c * n, n, 16)], rows_ref.at[y, pl.ds(c * n, n)],
                                   row_send.at[k, c], row_recv.at[k, c], device(core, x, py, z)))
        start_all(moves[c])
    own.wait()
    for c in range(CHUNKS):
        for copy in moves[c]:
            copy.wait_recv()
        blocks = [rows_ref[j, pl.ds(c * n, n), :] for j in range(4)]
        for i in range(4):
            part = dot(blocks[i], jnp.concatenate(blocks[i:], axis=1), 0, 0, None)
            for j in range(i, 4):
                b = BLOCKS.index((i, j))
                part_ref[128 * b:128 * b + 128, :] += part[:, 128 * (j - i):128 * (j - i) + 128]

    q = x * 4 + y

    def sizes(p):
        start, length = PARTS[p]
        return start, length // 2, length // 32, start // 2

    def swap(p):
        start, half, piece, hs = sizes(p)
        return remote(part_ref.at[at(start + (1 - core) * half, half)], from_core.at[pl.ds(hs, half)],
                      sum_send.at[p, 0, 0], sum_recv.at[p, 0, 0], sibling)

    def spread(p):
        start, half, piece, hs = sizes(p)
        return [remote(halves.at[at(hs + (px * 4 + py) * piece, piece)], from_plane.at[d, pl.ds(hs // 16, piece)],
                       sum_send.at[p, 1, d], sum_recv.at[p, 1, d], device(core, px, py, z)) for d, px, py in plane]

    def ring(p):
        start, half, piece, hs = sizes(p)
        mine = column.at[z, pl.ds(hs // 16, piece)]
        return [remote(mine, mine, sum_send.at[p, 2, d], sum_recv.at[p, 2, d], device(core, x, y, pz)) for d, pz in line]

    def back(p):
        start, half, piece, hs = sizes(p)
        mine = sum_ref.at[at(start + core * half + q * piece, piece)]
        return [remote(mine, mine, sum_send.at[p, 3, d], sum_recv.at[p, 3, d], device(core, px, py, z))
                for d, px, py in plane]

    def last(p):
        start, half, piece, hs = sizes(p)
        mine = sum_ref.at[at(start + core * half, half)]
        return remote(mine, mine, sum_send.at[p, 4, 0], sum_recv.at[p, 4, 0], sibling)

    def after_swap(p):
        start, half, piece, hs = sizes(p)
        swap(p).wait_recv()
        halves[pl.ds(hs, half), :] = part_ref[at(start + core * half, half), :] + from_core[pl.ds(hs, half), :]
        start_all(spread(p))

    def after_spread(p):
        start, half, piece, hs = sizes(p)
        total = halves[at(hs + q * piece, piece), :]
        for (d, _, _), copy in zip(plane, spread(p)):
            copy.wait_recv()
            total = total + from_plane[d, pl.ds(hs // 16, piece), :]
        column[z, pl.ds(hs // 16, piece), :] = total
        start_all(ring(p))

    def after_ring(p):
        start, half, piece, hs = sizes(p)
        for copy in ring(p):
            copy.wait_recv()
        total = column[0, pl.ds(hs // 16, piece), :]
        for k in range(1, 8):
            total = total + column[k, pl.ds(hs // 16, piece), :]
        sum_ref[at(start + core * half + q * piece, piece), :] = total
        start_all(back(p))

    def after_back(p):
        for copy in back(p):
            copy.wait_recv()
        last(p).start()

    def after_last(p):
        last(p).wait_recv()
        for b, (i, j) in enumerate(BLOCKS):
            if PARTS[p][0] <= 128 * b < sum(PARTS[p]):
                block = sum_ref[128 * b:128 * b + 128, :]
                g_ref[128 * i:128 * i + 128, 128 * j:128 * j + 128] = block
                if p == 0 and i != j:
                    g_ref[128 * j:128 * j + 128, 128 * i:128 * i + 128] = block.T

    swap(0).start()
    swap(1).start()
    after_swap(0)
    after_spread(0)
    after_swap(1)
    after_ring(0)
    after_spread(1)
    after_back(0)
    after_last(0)

    def between(step):
        for k, go_on in enumerate((after_ring, after_back)):
            @pl.when(step == k)
            def _():
                go_on(1)

    f0, f1 = level([g_ref.at[0:256, 0:256], g_ref.at[256:512, 256:512]], x_ref, between)
    g1_ref[0:128, 0:128] = dot(f0, dot(g_ref[0:256, 0:256], f0, 1, 0), 0, 0)
    g1_ref[128:256, 128:256] = dot(f1, dot(g_ref[256:512, 256:512], f1, 1, 0), 0, 0)
    after_last(1)
    cross = dot(f0, dot(g_ref[0:256, 256:512], f1, 1, 0), 0, 0)
    g1_ref[0:128, 128:256] = cross
    g1_ref[128:256, 0:128] = cross.T
    f, = level([g1_ref], x_ref)
    squares = jnp.sum(f * dot(g1_ref[...], f, 1, 0), axis=0, keepdims=True)
    energies = jnp.sqrt(squares + EPSILON)
    share = jnp.zeros((1, 32), F32)
    for j in range(4):
        share = jnp.where(y == j, energies[:, 32 * j:32 * j + 32], share)
    energy_ref[...] = share
    f = f * (1.0 / energies)
    weights = jnp.concatenate([dot(f[0:128], f0, 0, 1), dot(f[128:256], f1, 0, 1)], axis=1).astype(BF16)

    shares = []
    for c in range(CHUNKS):
        block = jnp.concatenate([rows_ref[j, pl.ds(c * n, n), :] for j in range(4)], axis=1)
        part = dot(weights, block, 1, 1, None).astype(BF16)
        for j in range(4):
            sent_ref[j, :, pl.ds(c * n, n)] = part[32 * j:32 * j + 32, :]
        for k in (2, 1, 3):
            py = lax.rem(y + k, 4)
            shares.append((py, c, remote(sent_ref.at[py, :, pl.ds(c * n, n)], got_ref.at[y, :, pl.ds(c * n, n)],
                                 out_send.at[k, c], out_recv.at[k, c], device(core, x, py, z))))
            shares[-1][-1].start()
    basis_ref[:, at(y * R, R, 128)] = sent_ref[y].astype(F32)
    for k in (1, 3, 2):
        for c in range(CHUNKS):
            py = lax.rem(y + k, 4)
            remote(got_ref.at[py, :, pl.ds(c * n, n)], got_ref.at[py, :, pl.ds(c * n, n)],
                   out_send.at[4 - k, c], out_recv.at[4 - k, c], device(core, x, py, z)).wait_recv()
            basis_ref[:, at(py * R + c * n, n, 128)] = got_ref[py, :, pl.ds(c * n, n)].astype(F32)
    for copies in moves:
        for copy in copies:
            copy.wait_send()
    for p in range(len(PARTS)):
        for copy in [swap(p), last(p)] + spread(p) + ring(p) + back(p):
            copy.wait_send()
    for _, c, copy in shares:
        copy.wait_send()


def body(snapshots):
    R = snapshots.shape[0] // 4
    total = sum(length for _, length in PARTS)
    basis, energies = pl.pallas_call(
        kernel,
        out_shape=(jax.ShapeDtypeStruct((32, 4 * R), F32), jax.ShapeDtypeStruct((1, 32), F32)),
        in_specs=[pl.BlockSpec(memory_space=pl.ANY)],
        out_specs=(pl.BlockSpec(memory_space=pltpu.VMEM),) * 2,
        scratch_shapes=[
            pltpu.VMEM((4, R, 128), BF16),
            pltpu.VMEM((total, 128), F32),
            pltpu.VMEM((total, 128), F32),
            pltpu.VMEM((total // 2, 128), F32),
            pltpu.VMEM((total // 2, 128), F32),
            pltpu.VMEM((16, total // 32, 128), F32),
            pltpu.VMEM((8, total // 32, 128), F32),
            pltpu.VMEM((512, 512), F32),
            pltpu.VMEM((256, 256), F32),
            pltpu.VMEM((2, 256, 128), F32),
            pltpu.VMEM((4, 32, R), BF16),
            pltpu.VMEM((4, 32, R), BF16),
            pltpu.SemaphoreType.DMA,
            pltpu.SemaphoreType.DMA((4, CHUNKS)),
            pltpu.SemaphoreType.DMA((4, CHUNKS)),
            pltpu.SemaphoreType.DMA((2, 5, 16)),
            pltpu.SemaphoreType.DMA((2, 5, 16)),
            pltpu.SemaphoreType.DMA((4, CHUNKS)),
            pltpu.SemaphoreType.DMA((4, CHUNKS)),
        ],
        compiler_params=pltpu.CompilerParams(collective_id=0, has_side_effects=True, vmem_limit_bytes=60 * 1024 * 1024),
    )(snapshots)
    return basis.T, energies.reshape(32)


def solution(mesh):
    return jax.shard_map(body, mesh=mesh, in_specs=(P("wide", "narrow"),), out_specs=(P("wide", "narrow"), P("narrow")),
                         check_vma=False)
```

```python
import functools

import jax
import jax.numpy as jnp
from jax import lax
from jax.experimental import pallas as pl
from jax.experimental.pallas import tpu as pltpu
from jax.sharding import PartitionSpec as P

MESH = pl.DeviceIdType.MESH
HI = lax.Precision.HIGHEST
F32 = jnp.float32
BF16 = jnp.bfloat16
SWEEPS = 3
EPSILON = 1e-6
BLOCKS = ((0, 0), (0, 1), (1, 1), (2, 2), (2, 3), (3, 3), (0, 2), (0, 3), (1, 2), (1, 3))
PARTS = ((0, 768), (768, 512))
CHUNKS = 4


def dot(a, b, ca, cb, precision=HI):
    return lax.dot_general(a, b, (((ca,), (cb,)), ((), ())), precision=precision, preferred_element_type=F32)


def thirds(a):
    high = a.astype(BF16)
    rest = a - high.astype(F32)
    middle = rest.astype(BF16)
    return high, middle, (rest - middle.astype(F32)).astype(BF16)


def short_dot(a, b):
    ah, am, al = thirds(a)
    bh, bm, bl = thirds(b)
    left = jnp.concatenate([ah, ah, am, am, ah, al], axis=0)
    right = jnp.concatenate([bh, bm, bh, bm, bl, bh], axis=0)
    return lax.dot_general(left, right, (((0,), (0,)), ((), ())), preferred_element_type=F32)


def inverse_cholesky(mats, outer=4, wide=2):
    n = 128
    lane = lax.broadcasted_iota(jnp.int32, (8, n), 1)
    sub = lax.broadcasted_iota(jnp.int32, (8, n), 0)
    S = [[a[8 * r:8 * r + 8, :] for r in range(n // 8)] for a in mats]
    M = range(len(mats))
    inverse_pivots = [[] for m in M]
    full = lambda row: jnp.broadcast_to(row, (8, n))
    for first in range(0, n // 8, outer):
        last = first + outer
        for p in range(first, last, wide):
            base = 8 * p
            inblock = (lane >= base) & (lane < base + 8 * wide)
            E = [[{r: full(S[m][r][:, base + j:base + j + 1]) for r in range(p + j // 8, last)}
                  for j in range(8 * wide)] for m in M]
            for m in M:
                for r in range(p, last):
                    fill = jnp.where(lane - 8 * r == sub, 1.0, 0.0) if r < p + wide else 0.0
                    S[m][r] = jnp.where(inblock, fill, S[m][r])
            scale = [[jnp.zeros((8, n), F32)] * wide for m in M]
            for k in range(8 * wide):
                top, row = p + k // 8, k % 8
                inv = [1.0 / full(E[m][k][top][row:row + 1, :]) for m in M]
                for m in M:
                    scale[m][k // 8] = jnp.where(sub == row, inv[m], scale[m][k // 8])
                    pivots = {j: full(E[m][k][p + j // 8][j % 8:j % 8 + 1, :]) for j in range(k + 1, 8 * wide)}
                    pivot_row = full(S[m][top][row:row + 1, :])
                    for r in range(top, last):
                        mult = E[m][k][r] * inv[m]
                        if r == top:
                            mult = jnp.where(sub > row, mult, 0.0)
                        for j in range(k + 1, 8 * wide):
                            if r >= p + j // 8:
                                E[m][j][r] = E[m][j][r] - mult * pivots[j]
                        S[m][r] = S[m][r] - mult * pivot_row
            for m in M:
                inverse_pivots[m] += scale[m]
        if last < n // 8:
            for m in M:
                left = jnp.concatenate([jnp.where(lane >= 8 * last, S[m][p] * inverse_pivots[m][p], 0.0)
                                        for p in range(first, last)], axis=0)
                right = jnp.concatenate(
                    [jnp.where((lane >= 8 * last) | (lane < 8 * (p - (p - first) % wide + wide)), S[m][p], 0.0)
                     for p in range(first, last)], axis=0)
                update = short_dot(left, right)
                outside = (lane < 8 * first) | (lane >= 8 * last)
                for r in range(last, n // 8):
                    S[m][r] = jnp.where(outside, S[m][r], 0.0) - update[8 * r:8 * r + 8, :]
    return [jnp.concatenate([jnp.where(lane <= sub + 8 * r, S[m][r] * jnp.sqrt(inverse_pivots[m][r]), 0.0) for r in range(n // 8)], axis=0) for m in M]


def device(core, x, y, z):
    return {"wide": (z * 4 + x) * 2 + core, "narrow": y}


def remote(src, dst, send, recv, peer):
    return pltpu.make_async_remote_copy(src_ref=src, dst_ref=dst, send_sem=send, recv_sem=recv,
                                        device_id=peer, device_id_type=MESH)


def at(start, size, align=8):
    return pl.ds(pl.multiple_of(start, align), size)


def start_all(copies):
    for copy in copies:
        copy.start()


def arrived(like, sem):
    pltpu.make_async_copy(like, like, sem).wait()


def level(grams, y_ref, between=None):
    for m, g in enumerate(grams):
        y_ref[m] = (g[:, 0:128] + g[:, 128:256]) * F32(0.5 ** 0.5)

    def sweep(step, carry):
        ys = [y_ref[m] for m in range(len(grams))]
        linv = inverse_cholesky([dot(v, v, 0, 0) for v in ys])
        ahead = [jnp.where(step == SWEEPS - 1, v, dot(g[...], v, 1, 0)) for g, v in zip(grams, ys)]
        for m, v in enumerate(ahead):
            y_ref[m] = dot(v, linv[m], 1, 1)
        if between is not None:
            between(step)
        return carry

    lax.fori_loop(0, SWEEPS, sweep, 0)
    return [y_ref[m].astype(BF16).astype(F32) for m in range(len(grams))]


def kernel(s_ref, basis_ref, energy_ref, rows_ref, part_ref, sum_ref, from_core, halves, from_plane, column,
           g_ref, g1_ref, x_ref, sent_ref, got_ref,
           own_sem, row_send, row_recv, sum_send, sum_recv, out_send, out_recv):
    w = lax.axis_index("wide")
    y = lax.axis_index("narrow")
    core, x, z = lax.rem(w, 2), lax.rem(lax.div(w, 2), 4), lax.div(w, 8)
    n = rows_ref.shape[2]
    R = n * CHUNKS
    sibling = device(1 - core, x, y, z)
    plane = [(d, lax.rem(x + d // 4, 4), lax.rem(y + d % 4, 4)) for d in range(1, 16)]
    line = [(d, lax.rem(z + d, 8)) for d in range(1, 8)]

    barrier = pltpu.get_barrier_semaphore()
    peers = [device(core, x, y, pz) for d, pz in sorted(line, key=lambda v: abs(v[0] - 4))]
    peers += [device(core, px, py, z) for d, px, py in sorted(plane, key=lambda v: abs(v[0] // 4 - 2) + abs(v[0] % 4 - 2))]
    peers += [sibling]
    for peer in peers:
        pl.semaphore_signal(barrier, inc=1, device_id=peer, device_id_type=MESH)
    for c in range(CHUNKS):
        pltpu.make_async_copy(s_ref.at[at(y * R + c * n, n, 16)], rows_ref.at[c, y], own_sem).start()
    part_ref[...] = jnp.zeros_like(part_ref)
    pl.semaphore_wait(barrier, len(peers))

    for c in range(CHUNKS):
        for k in (2, 1, 3):
            py = lax.rem(y + k, 4)
            remote(s_ref.at[at(py * R + c * n, n, 16)], rows_ref.at[c, y], row_send, row_recv.at[c],
                   device(core, x, py, z)).start()
    arrived(rows_ref.at[0], own_sem)
    for c in range(CHUNKS):
        arrived(rows_ref.at[c, pl.ds(0, 3)], row_recv.at[c])
        blocks = [rows_ref[c, j] for j in range(4)]
        for i in range(4):
            part = dot(blocks[i], jnp.concatenate(blocks[i:], axis=1), 0, 0, None)
            for j in range(i, 4):
                b = BLOCKS.index((i, j))
                part_ref[128 * b:128 * b + 128, :] += part[:, 128 * (j - i):128 * (j - i) + 128]

    q = x * 4 + y

    def sizes(p):
        start, length = PARTS[p]
        return start, length // 2, length // 32, start // 2

    def swap(p):
        start, half, piece, hs = sizes(p)
        remote(part_ref.at[at(start + (1 - core) * half, half)], from_core.at[pl.ds(hs, half)],
               sum_send.at[p, 0], sum_recv.at[p, 0], sibling).start()

    def after_swap(p):
        start, half, piece, hs = sizes(p)
        arrived(from_core.at[pl.ds(hs, half)], sum_recv.at[p, 0])
        halves[pl.ds(hs, half), :] = part_ref[at(start + core * half, half), :] + from_core[pl.ds(hs, half), :]
        for d, px, py in plane:
            remote(halves.at[at(hs + (px * 4 + py) * piece, piece)], from_plane.at[d, pl.ds(hs // 16, piece)],
                   sum_send.at[p, 1], sum_recv.at[p, 1], device(core, px, py, z)).start()

    def after_spread(p):
        start, half, piece, hs = sizes(p)
        arrived(from_plane.at[pl.ds(1, 15), pl.ds(hs // 16, piece)], sum_recv.at[p, 1])
        total = halves[at(hs + q * piece, piece), :]
        for d in range(1, 16):
            total = total + from_plane[d, pl.ds(hs // 16, piece), :]
        mine = column.at[z, pl.ds(hs // 16, piece)]
        mine[...] = total
        for d, pz in line:
            remote(mine, mine, sum_send.at[p, 2], sum_recv.at[p, 2], device(core, x, y, pz)).start()

    def after_ring(p):
        start, half, piece, hs = sizes(p)
        arrived(column.at[pl.ds(0, 7), pl.ds(hs // 16, piece)], sum_recv.at[p, 2])
        total = column[0, pl.ds(hs // 16, piece), :]
        for k in range(1, 8):
            total = total + column[k, pl.ds(hs // 16, piece), :]
        mine = sum_ref.at[at(start + core * half + q * piece, piece)]
        mine[...] = total
        for d, px, py in plane:
            remote(mine, mine, sum_send.at[p, 3], sum_recv.at[p, 3], device(core, px, py, z)).start()

    def after_back(p):
        start, half, piece, hs = sizes(p)
        arrived(sum_ref.at[pl.ds(start, 15 * piece)], sum_recv.at[p, 3])
        mine = sum_ref.at[at(start + core * half, half)]
        remote(mine, mine, sum_send.at[p, 4], sum_recv.at[p, 4], sibling).start()

    def after_last(p):
        start, half, piece, hs = sizes(p)
        arrived(sum_ref.at[pl.ds(start, half)], sum_recv.at[p, 4])
        for b, (i, j) in enumerate(BLOCKS):
            if PARTS[p][0] <= 128 * b < sum(PARTS[p]):
                block = sum_ref[128 * b:128 * b + 128, :]
                g_ref[128 * i:128 * i + 128, 128 * j:128 * j + 128] = block
                if p == 0 and i != j:
                    g_ref[128 * j:128 * j + 128, 128 * i:128 * i + 128] = block.T

    def all_left(p):
        start, half, piece, hs = sizes(p)
        arrived(from_core.at[pl.ds(hs, half)], sum_send.at[p, 0])
        arrived(from_plane.at[pl.ds(1, 15), pl.ds(hs // 16, piece)], sum_send.at[p, 1])
        arrived(column.at[pl.ds(0, 7), pl.ds(hs // 16, piece)], sum_send.at[p, 2])
        arrived(sum_ref.at[pl.ds(start, 15 * piece)], sum_send.at[p, 3])
        arrived(sum_ref.at[pl.ds(start, half)], sum_send.at[p, 4])

    swap(0)
    swap(1)
    after_swap(0)
    after_spread(0)
    after_swap(1)
    after_ring(0)
    after_spread(1)
    after_back(0)
    after_last(0)

    def between(step):
        for k, go_on in enumerate((after_ring, after_back)):
            @pl.when(step == k)
            def _():
                go_on(1)

    f0, f1 = level([g_ref.at[0:256, 0:256], g_ref.at[256:512, 256:512]], x_ref, between)
    g1_ref[0:128, 0:128] = dot(f0, dot(g_ref[0:256, 0:256], f0, 1, 0), 0, 0)
    g1_ref[128:256, 128:256] = dot(f1, dot(g_ref[256:512, 256:512], f1, 1, 0), 0, 0)
    after_last(1)
    cross = dot(f0, dot(g_ref[0:256, 256:512], f1, 1, 0), 0, 0)
    g1_ref[0:128, 128:256] = cross
    g1_ref[128:256, 0:128] = cross.T
    f, = level([g1_ref], x_ref)
    weights = jnp.concatenate([dot(f[0:128].astype(BF16), f0.astype(BF16), 0, 1, None),
                               dot(f[128:256].astype(BF16), f1.astype(BF16), 0, 1, None)], axis=1).astype(BF16)
    squares = dot(f, dot(g1_ref[...], f, 1, 0), 0, 0)
    diagonal = lax.broadcasted_iota(jnp.int32, (128, 128), 0) == lax.broadcasted_iota(jnp.int32, (128, 128), 1)
    squares = jnp.where(diagonal, squares, 0.0)
    inverse = 1.0 / jnp.sqrt(jnp.sum(squares, axis=1, keepdims=True) + EPSILON)
    energies = jnp.sqrt(jnp.sum(squares, axis=0, keepdims=True) + EPSILON)
    share = jnp.zeros((1, 32), F32)
    for j in range(4):
        share = jnp.where(y == j, energies[:, 32 * j:32 * j + 32], share)
    energy_ref[...] = share

    for c in range(CHUNKS):
        block = jnp.concatenate([rows_ref[c, j] for j in range(4)], axis=1)
        part = (dot(weights, block, 1, 1, None) * inverse).astype(BF16)
        for j in range(4):
            sent_ref[c, j] = part[32 * j:32 * j + 32, :]
        for k in (2, 1, 3):
            py = lax.rem(y + k, 4)
            remote(sent_ref.at[c, py], got_ref.at[c, y], out_send, out_recv.at[c], device(core, x, py, z)).start()
    for c in range(CHUNKS):
        basis_ref[:, at(y * R + c * n, n, 128)] = sent_ref[c, y].astype(F32)
    for c in range(CHUNKS):
        arrived(got_ref.at[c, pl.ds(0, 3)], out_recv.at[c])
        for k in (1, 2, 3):
            py = lax.rem(y + k, 4)
            basis_ref[:, at(py * R + c * n, n, 128)] = got_ref[c, py].astype(F32)
    arrived(rows_ref.at[pl.ds(0, 3)], row_send)
    for p in range(len(PARTS)):
        all_left(p)
    arrived(got_ref.at[pl.ds(0, 3)], out_send)


def body(snapshots):
    R = snapshots.shape[0] // 4
    total = sum(length for _, length in PARTS)
    basis, energies = pl.pallas_call(
        kernel,
        out_shape=(jax.ShapeDtypeStruct((32, 4 * R), F32), jax.ShapeDtypeStruct((1, 32), F32)),
        in_specs=[pl.BlockSpec(memory_space=pl.ANY)],
        out_specs=(pl.BlockSpec(memory_space=pltpu.VMEM),) * 2,
        scratch_shapes=[
            pltpu.VMEM((CHUNKS, 4, R // CHUNKS, 128), BF16),
            pltpu.VMEM((total, 128), F32),
            pltpu.VMEM((total, 128), F32),
            pltpu.VMEM((total // 2, 128), F32),
            pltpu.VMEM((total // 2, 128), F32),
            pltpu.VMEM((16, total // 32, 128), F32),
            pltpu.VMEM((8, total // 32, 128), F32),
            pltpu.VMEM((512, 512), F32),
            pltpu.VMEM((256, 256), F32),
            pltpu.VMEM((2, 256, 128), F32),
            pltpu.VMEM((CHUNKS, 4, 32, R // CHUNKS), BF16),
            pltpu.VMEM((CHUNKS, 4, 32, R // CHUNKS), BF16),
            pltpu.SemaphoreType.DMA,
            pltpu.SemaphoreType.DMA,
            pltpu.SemaphoreType.DMA((CHUNKS,)),
            pltpu.SemaphoreType.DMA((2, 5)),
            pltpu.SemaphoreType.DMA((2, 5)),
            pltpu.SemaphoreType.DMA,
            pltpu.SemaphoreType.DMA((CHUNKS,)),
        ],
        compiler_params=pltpu.CompilerParams(collective_id=0, has_side_effects=True, vmem_limit_bytes=103 * 512 * 1024),
    )(snapshots)
    return basis.T, energies.reshape(32)


def solution(mesh):
    return jax.shard_map(body, mesh=mesh, in_specs=(P("wide", "narrow"),), out_specs=(P("wide", "narrow"), P("narrow")),
                         check_vma=False)
```

```python
import functools

import jax
import jax.numpy as jnp
from jax import lax
from jax.experimental import pallas as pl
from jax.experimental.pallas import tpu as pltpu
from jax.sharding import PartitionSpec as P

MESH = pl.DeviceIdType.MESH
HI = lax.Precision.HIGHEST
F32 = jnp.float32
BF16 = jnp.bfloat16
SWEEPS = 3
EPSILON = 1e-6
BLOCKS = ((0, 0), (0, 1), (1, 1), (2, 2), (2, 3), (3, 3), (0, 2), (0, 3), (1, 2), (1, 3))
PARTS = ((0, 768), (768, 512))
CHUNKS = 4


def dot(a, b, ca, cb, precision=HI):
    return lax.dot_general(a, b, (((ca,), (cb,)), ((), ())), precision=precision, preferred_element_type=F32)


def thirds(a):
    high = a.astype(BF16)
    rest = a - high.astype(F32)
    middle = rest.astype(BF16)
    return high, middle, (rest - middle.astype(F32)).astype(BF16)


def short_dot(a, b):
    ah, am, al = thirds(a)
    bh, bm, bl = thirds(b)
    left = jnp.concatenate([ah, ah, am, am, ah, al], axis=0)
    right = jnp.concatenate([bh, bm, bh, bm, bl, bh], axis=0)
    return lax.dot_general(left, right, (((0,), (0,)), ((), ())), preferred_element_type=F32)


def inverse_cholesky(mats, outer=4, wide=2):
    n = 128
    lane = lax.broadcasted_iota(jnp.int32, (8, n), 1)
    sub = lax.broadcasted_iota(jnp.int32, (8, n), 0)
    S = [[a[8 * r:8 * r + 8, :] for r in range(n // 8)] for a in mats]
    M = range(len(mats))
    inverse_pivots = [[] for m in M]
    full = lambda row: jnp.broadcast_to(row, (8, n))
    for first in range(0, n // 8, outer):
        last = first + outer
        for p in range(first, last, wide):
            base = 8 * p
            inblock = (lane >= base) & (lane < base + 8 * wide)
            E = [[{r: full(S[m][r][:, base + j:base + j + 1]) for r in range(p + j // 8, last)}
                  for j in range(8 * wide)] for m in M]
            for m in M:
                for r in range(p, last):
                    fill = jnp.where(lane - 8 * r == sub, 1.0, 0.0) if r < p + wide else 0.0
                    S[m][r] = jnp.where(inblock, fill, S[m][r])
            scale = [[jnp.zeros((8, n), F32)] * wide for m in M]
            for k in range(8 * wide):
                top, row = p + k // 8, k % 8
                inv = [1.0 / full(E[m][k][top][row:row + 1, :]) for m in M]
                for m in M:
                    scale[m][k // 8] = jnp.where(sub == row, inv[m], scale[m][k // 8])
                    pivots = {j: full(E[m][k][p + j // 8][j % 8:j % 8 + 1, :]) for j in range(k + 1, 8 * wide)}
                    pivot_row = full(S[m][top][row:row + 1, :])
                    for r in range(top, last):
                        mult = E[m][k][r] * inv[m]
                        if r == top:
                            mult = jnp.where(sub > row, mult, 0.0)
                        for j in range(k + 1, 8 * wide):
                            if r >= p + j // 8:
                                E[m][j][r] = E[m][j][r] - mult * pivots[j]
                        S[m][r] = S[m][r] - mult * pivot_row
            for m in M:
                inverse_pivots[m] += scale[m]
        if last < n // 8:
            for m in M:
                left = jnp.concatenate([jnp.where(lane >= 8 * last, S[m][p] * inverse_pivots[m][p], 0.0)
                                        for p in range(first, last)], axis=0)
                right = jnp.concatenate(
                    [jnp.where((lane >= 8 * last) | (lane < 8 * (p - (p - first) % wide + wide)), S[m][p], 0.0)
                     for p in range(first, last)], axis=0)
                update = short_dot(left, right)
                outside = (lane < 8 * first) | (lane >= 8 * last)
                for r in range(last, n // 8):
                    S[m][r] = jnp.where(outside, S[m][r], 0.0) - update[8 * r:8 * r + 8, :]
    return [jnp.concatenate([jnp.where(lane <= sub + 8 * r, S[m][r] * jnp.sqrt(inverse_pivots[m][r]), 0.0) for r in range(n // 8)], axis=0) for m in M]


def device(core, x, y, z):
    return {"wide": (z * 4 + x) * 2 + core, "narrow": y}


def remote(src, dst, send, recv, peer):
    return pltpu.make_async_remote_copy(src_ref=src, dst_ref=dst, send_sem=send, recv_sem=recv,
                                        device_id=peer, device_id_type=MESH)


def at(start, size, align=8):
    return pl.ds(pl.multiple_of(start, align), size)


def start_all(copies):
    for copy in copies:
        copy.start()


def arrived(like, sem):
    pltpu.make_async_copy(like, like, sem).wait()


def level(gram, y_ref, between=None):
    y_ref[...] = (gram[:, 0:128] + gram[:, 128:256]) * F32(0.5 ** 0.5)

    def sweep(step, carry):
        tall = y_ref[...]
        linv, = inverse_cholesky([dot(tall, tall, 0, 0)])
        ahead = jnp.where(step == SWEEPS - 1, tall, dot(gram[...], tall, 1, 0))
        y_ref[...] = dot(ahead, linv, 1, 1)
        if between is not None:
            between(step)
        return carry

    lax.fori_loop(0, SWEEPS, sweep, 0)
    return y_ref[...].astype(BF16)


def kernel(s_ref, basis_ref, energy_ref, rows_ref, part_ref, sum_ref, from_core, halves, from_plane, column,
           g_ref, g1_ref, y_ref, f_ref, d_ref, sent_ref, got_ref,
           own_sem, row_send, row_recv, sum_send, sum_recv, pair_send, pair_recv, out_send, out_recv):
    w = lax.axis_index("wide")
    y = lax.axis_index("narrow")
    core, x, z = lax.rem(w, 2), lax.rem(lax.div(w, 2), 4), lax.div(w, 8)
    n = rows_ref.shape[2]
    R = n * CHUNKS
    sibling = device(1 - core, x, y, z)
    plane = [(d, lax.rem(x + d // 4, 4), lax.rem(y + d % 4, 4)) for d in range(1, 16)]
    line = [(d, lax.rem(z + d, 8)) for d in range(1, 8)]

    barrier = pltpu.get_barrier_semaphore()
    peers = [device(core, x, y, pz) for d, pz in sorted(line, key=lambda v: abs(v[0] - 4))]
    peers += [device(core, px, py, z) for d, px, py in sorted(plane, key=lambda v: abs(v[0] // 4 - 2) + abs(v[0] % 4 - 2))]
    peers += [sibling]
    for peer in peers:
        pl.semaphore_signal(barrier, inc=1, device_id=peer, device_id_type=MESH)
    for c in range(CHUNKS):
        pltpu.make_async_copy(s_ref.at[at(y * R + c * n, n, 16)], rows_ref.at[c, y], own_sem).start()
    part_ref[...] = jnp.zeros_like(part_ref)
    pl.semaphore_wait(barrier, len(peers))

    for c in range(CHUNKS):
        for k in (2, 1, 3):
            py = lax.rem(y + k, 4)
            remote(s_ref.at[at(py * R + c * n, n, 16)], rows_ref.at[c, y], row_send, row_recv.at[c],
                   device(core, x, py, z)).start()
    arrived(rows_ref.at[0], own_sem)
    for c in range(CHUNKS):
        arrived(rows_ref.at[c, pl.ds(0, 3)], row_recv.at[c])
        blocks = [rows_ref[c, j] for j in range(4)]
        for i in range(4):
            part = dot(blocks[i], jnp.concatenate(blocks[i:], axis=1), 0, 0, None)
            for j in range(i, 4):
                b = BLOCKS.index((i, j))
                part_ref[128 * b:128 * b + 128, :] += part[:, 128 * (j - i):128 * (j - i) + 128]

    q = x * 4 + y

    def sizes(p):
        start, length = PARTS[p]
        return start, length // 2, length // 32, start // 2

    def swap(p):
        start, half, piece, hs = sizes(p)
        remote(part_ref.at[at(start + (1 - core) * half, half)], from_core.at[pl.ds(hs, half)],
               sum_send.at[p, 0], sum_recv.at[p, 0], sibling).start()

    def after_swap(p):
        start, half, piece, hs = sizes(p)
        arrived(from_core.at[pl.ds(hs, half)], sum_recv.at[p, 0])
        halves[pl.ds(hs, half), :] = part_ref[at(start + core * half, half), :] + from_core[pl.ds(hs, half), :]
        for d, px, py in plane:
            remote(halves.at[at(hs + (px * 4 + py) * piece, piece)], from_plane.at[d, pl.ds(hs // 16, piece)],
                   sum_send.at[p, 1], sum_recv.at[p, 1], device(core, px, py, z)).start()

    def after_spread(p):
        start, half, piece, hs = sizes(p)
        arrived(from_plane.at[pl.ds(1, 15), pl.ds(hs // 16, piece)], sum_recv.at[p, 1])
        total = halves[at(hs + q * piece, piece), :]
        for d in range(1, 16):
            total = total + from_plane[d, pl.ds(hs // 16, piece), :]
        mine = column.at[z, pl.ds(hs // 16, piece)]
        mine[...] = total
        for d, pz in line:
            remote(mine, mine, sum_send.at[p, 2], sum_recv.at[p, 2], device(core, x, y, pz)).start()

    def after_ring(p):
        start, half, piece, hs = sizes(p)
        arrived(column.at[pl.ds(0, 7), pl.ds(hs // 16, piece)], sum_recv.at[p, 2])
        total = column[0, pl.ds(hs // 16, piece), :]
        for k in range(1, 8):
            total = total + column[k, pl.ds(hs // 16, piece), :]
        mine = sum_ref.at[at(start + core * half + q * piece, piece)]
        mine[...] = total
        for d, px, py in plane:
            remote(mine, mine, sum_send.at[p, 3], sum_recv.at[p, 3], device(core, px, py, z)).start()

    def after_back(p):
        start, half, piece, hs = sizes(p)
        arrived(sum_ref.at[pl.ds(start, 15 * piece)], sum_recv.at[p, 3])

    def last(p):
        start, half, piece, hs = sizes(p)
        mine = sum_ref.at[at(start + core * half, half)]
        remote(mine, mine, sum_send.at[p, 4], sum_recv.at[p, 4], sibling).start()

    def after_last(p):
        start, half, piece, hs = sizes(p)
        arrived(sum_ref.at[pl.ds(start, half)], sum_recv.at[p, 4])

    def all_left(p):
        start, half, piece, hs = sizes(p)
        arrived(from_core.at[pl.ds(hs, half)], sum_send.at[p, 0])
        arrived(from_plane.at[pl.ds(1, 15), pl.ds(hs // 16, piece)], sum_send.at[p, 1])
        arrived(column.at[pl.ds(0, 7), pl.ds(hs // 16, piece)], sum_send.at[p, 2])
        arrived(sum_ref.at[pl.ds(start, 15 * piece)], sum_send.at[p, 3])
        if p == 1:
            arrived(sum_ref.at[pl.ds(start, half)], sum_send.at[p, 4])

    swap(0)
    swap(1)
    after_swap(0)
    after_spread(0)
    after_swap(1)
    after_ring(0)
    after_spread(1)
    after_back(0)

    def between(step):
        @pl.when(step == 0)
        def _():
            after_ring(1)

        @pl.when(step == 1)
        def _():
            after_back(1)
            last(1)

    low, cross, high = [sum_ref[at(core * 384 + 128 * k, 128), :] for k in range(3)]
    g_ref[0:128, 0:128] = low
    g_ref[0:128, 128:256] = cross
    g_ref[128:256, 0:128] = cross.T
    g_ref[128:256, 128:256] = high
    own_factor = level(g_ref, y_ref, between)
    f_ref[core] = own_factor
    mine = f_ref.at[core]
    remote(mine, mine, pair_send.at[0], pair_recv.at[0], sibling).start()
    wide = own_factor.astype(F32)
    d_ref[core] = dot(wide, dot(g_ref[...], wide, 1, 0), 0, 0)
    block = d_ref.at[core]
    remote(block, block, pair_send.at[1], pair_recv.at[1], sibling).start()
    after_last(1)
    between_pairs = jnp.concatenate(
        [jnp.concatenate([sum_ref[768 + 256 * i + 128 * j:896 + 256 * i + 128 * j, :] for j in range(2)], axis=1)
         for i in range(2)], axis=0)
    arrived(f_ref.at[0], pair_recv.at[0])
    f0, f1 = f_ref[0], f_ref[1]
    cross = dot(f0.astype(F32), dot(between_pairs, f1.astype(F32), 1, 0), 0, 0)
    arrived(d_ref.at[0], pair_recv.at[1])
    g1_ref[0:128, 0:128] = d_ref[0]
    g1_ref[0:128, 128:256] = cross
    g1_ref[128:256, 0:128] = cross.T
    g1_ref[128:256, 128:256] = d_ref[1]
    f = level(g1_ref, y_ref)
    weights = jnp.concatenate([dot(f[0:128], f0, 0, 1, None), dot(f[128:256], f1, 0, 1, None)], axis=1).astype(BF16)
    wide = f.astype(F32)
    squares = dot(wide, dot(g1_ref[...], wide, 1, 0), 0, 0)
    diagonal = lax.broadcasted_iota(jnp.int32, (128, 128), 0) == lax.broadcasted_iota(jnp.int32, (128, 128), 1)
    squares = jnp.where(diagonal, squares, 0.0)
    inverse = 1.0 / jnp.sqrt(jnp.sum(squares, axis=1, keepdims=True) + EPSILON)
    energies = jnp.sqrt(jnp.sum(squares, axis=0, keepdims=True) + EPSILON)
    share = jnp.zeros((1, 32), F32)
    for j in range(4):
        share = jnp.where(y == j, energies[:, 32 * j:32 * j + 32], share)
    energy_ref[...] = share

    for c in range(CHUNKS):
        block = jnp.concatenate([rows_ref[c, j] for j in range(4)], axis=1)
        part = (dot(weights, block, 1, 1, None) * inverse).astype(BF16)
        for j in range(4):
            sent_ref[c, j] = part[32 * j:32 * j + 32, :]
        for k in (2, 1, 3):
            py = lax.rem(y + k, 4)
            remote(sent_ref.at[c, py], got_ref.at[c, y], out_send, out_recv.at[c], device(core, x, py, z)).start()
    for c in range(CHUNKS):
        basis_ref[:, at(y * R + c * n, n, 128)] = sent_ref[c, y].astype(F32)
    for c in range(CHUNKS):
        arrived(got_ref.at[c, pl.ds(0, 3)], out_recv.at[c])
        for k in (1, 2, 3):
            py = lax.rem(y + k, 4)
            basis_ref[:, at(py * R + c * n, n, 128)] = got_ref[c, py].astype(F32)
    arrived(rows_ref.at[pl.ds(0, 3)], row_send)
    for p in range(len(PARTS)):
        all_left(p)
    arrived(f_ref.at[0], pair_send.at[0])
    arrived(d_ref.at[0], pair_send.at[1])
    arrived(got_ref.at[pl.ds(0, 3)], out_send)


def body(snapshots):
    R = snapshots.shape[0] // 4
    total = sum(length for _, length in PARTS)
    basis, energies = pl.pallas_call(
        kernel,
        out_shape=(jax.ShapeDtypeStruct((32, 4 * R), F32), jax.ShapeDtypeStruct((1, 32), F32)),
        in_specs=[pl.BlockSpec(memory_space=pl.ANY)],
        out_specs=(pl.BlockSpec(memory_space=pltpu.VMEM),) * 2,
        scratch_shapes=[
            pltpu.VMEM((CHUNKS, 4, R // CHUNKS, 128), BF16),
            pltpu.VMEM((total, 128), F32),
            pltpu.VMEM((total, 128), F32),
            pltpu.VMEM((total // 2, 128), F32),
            pltpu.VMEM((total // 2, 128), F32),
            pltpu.VMEM((16, total // 32, 128), F32),
            pltpu.VMEM((8, total // 32, 128), F32),
            pltpu.VMEM((256, 256), F32),
            pltpu.VMEM((256, 256), F32),
            pltpu.VMEM((256, 128), F32),
            pltpu.VMEM((2, 256, 128), BF16),
            pltpu.VMEM((2, 128, 128), F32),
            pltpu.VMEM((CHUNKS, 4, 32, R // CHUNKS), BF16),
            pltpu.VMEM((CHUNKS, 4, 32, R // CHUNKS), BF16),
            pltpu.SemaphoreType.DMA,
            pltpu.SemaphoreType.DMA,
            pltpu.SemaphoreType.DMA((CHUNKS,)),
            pltpu.SemaphoreType.DMA((2, 5)),
            pltpu.SemaphoreType.DMA((2, 5)),
            pltpu.SemaphoreType.DMA((2,)),
            pltpu.SemaphoreType.DMA((2,)),
            pltpu.SemaphoreType.DMA,
            pltpu.SemaphoreType.DMA((CHUNKS,)),
        ],
        compiler_params=pltpu.CompilerParams(collective_id=0, has_side_effects=True, vmem_limit_bytes=103 * 512 * 1024),
    )(snapshots)
    return basis.T, energies.reshape(32)


def solution(mesh):
    return jax.shard_map(body, mesh=mesh, in_specs=(P("wide", "narrow"),), out_specs=(P("wide", "narrow"), P("narrow")),
                         check_vma=False)
```

```python
import functools

import jax
import jax.numpy as jnp
from jax import lax
from jax.experimental import pallas as pl
from jax.experimental.pallas import tpu as pltpu
from jax.sharding import PartitionSpec as P

MESH = pl.DeviceIdType.MESH
HI = lax.Precision.HIGHEST
F32 = jnp.float32
BF16 = jnp.bfloat16
SWEEPS = 3
EPSILON = 1e-6
BLOCKS = ((0, 1), (2, 3), (0, 2), (0, 3), (1, 2), (1, 3))
PARTS = ((0, 256), (256, 512))
TILES = 8
CHUNKS = 4


def dot(a, b, ca, cb, precision=HI):
    return lax.dot_general(a, b, (((ca,), (cb,)), ((), ())), precision=precision, preferred_element_type=F32)


def thirds(a):
    high = a.astype(BF16)
    rest = a - high.astype(F32)
    middle = rest.astype(BF16)
    return high, middle, (rest - middle.astype(F32)).astype(BF16)


def short_dot(a, b):
    ah, am, al = thirds(a)
    bh, bm, bl = thirds(b)
    left = jnp.concatenate([ah, ah, am, am, ah, al], axis=0)
    right = jnp.concatenate([bh, bm, bh, bm, bl, bh], axis=0)
    return lax.dot_general(left, right, (((0,), (0,)), ((), ())), preferred_element_type=F32)


def inverse_cholesky(mats, outer=4, wide=2):
    n = 128
    lane = lax.broadcasted_iota(jnp.int32, (8, n), 1)
    sub = lax.broadcasted_iota(jnp.int32, (8, n), 0)
    S = [[a[8 * r:8 * r + 8, :] for r in range(n // 8)] for a in mats]
    M = range(len(mats))
    inverse_pivots = [[] for m in M]
    full = lambda row: jnp.broadcast_to(row, (8, n))
    for first in range(0, n // 8, outer):
        last = first + outer
        for p in range(first, last, wide):
            base = 8 * p
            inblock = (lane >= base) & (lane < base + 8 * wide)
            E = [[{r: full(S[m][r][:, base + j:base + j + 1]) for r in range(p + j // 8, last)}
                  for j in range(8 * wide)] for m in M]
            for m in M:
                for r in range(p, last):
                    fill = jnp.where(lane - 8 * r == sub, 1.0, 0.0) if r < p + wide else 0.0
                    S[m][r] = jnp.where(inblock, fill, S[m][r])
            scale = [[jnp.zeros((8, n), F32)] * wide for m in M]
            for k in range(8 * wide):
                top, row = p + k // 8, k % 8
                inv = [1.0 / full(E[m][k][top][row:row + 1, :]) for m in M]
                for m in M:
                    scale[m][k // 8] = jnp.where(sub == row, inv[m], scale[m][k // 8])
                    pivots = {j: full(E[m][k][p + j // 8][j % 8:j % 8 + 1, :]) for j in range(k + 1, 8 * wide)}
                    pivot_row = full(S[m][top][row:row + 1, :])
                    for r in range(top, last):
                        mult = E[m][k][r] * inv[m]
                        if r == top:
                            mult = jnp.where(sub > row, mult, 0.0)
                        for j in range(k + 1, 8 * wide):
                            if r >= p + j // 8:
                                E[m][j][r] = E[m][j][r] - mult * pivots[j]
                        S[m][r] = S[m][r] - mult * pivot_row
            for m in M:
                inverse_pivots[m] += scale[m]
        if last < n // 8:
            for m in M:
                left = jnp.concatenate([jnp.where(lane >= 8 * last, S[m][p] * inverse_pivots[m][p], 0.0)
                                        for p in range(first, last)], axis=0)
                right = jnp.concatenate(
                    [jnp.where((lane >= 8 * last) | (lane < 8 * (p - (p - first) % wide + wide)), S[m][p], 0.0)
                     for p in range(first, last)], axis=0)
                update = short_dot(left, right)
                outside = (lane < 8 * first) | (lane >= 8 * last)
                for r in range(last, n // 8):
                    S[m][r] = jnp.where(outside, S[m][r], 0.0) - update[8 * r:8 * r + 8, :]
    return [jnp.concatenate([jnp.where(lane <= sub + 8 * r, S[m][r] * jnp.sqrt(inverse_pivots[m][r]), 0.0) for r in range(n // 8)], axis=0) for m in M]


def device(core, x, y, z):
    return {"wide": (z * 4 + x) * 2 + core, "narrow": y}


def remote(src, dst, send, recv, peer):
    return pltpu.make_async_remote_copy(src_ref=src, dst_ref=dst, send_sem=send, recv_sem=recv,
                                        device_id=peer, device_id_type=MESH)


def at(start, size, align=8):
    return pl.ds(pl.multiple_of(start, align), size)


def start_all(copies):
    for copy in copies:
        copy.start()


def arrived(like, sem):
    pltpu.make_async_copy(like, like, sem).wait()


def level(gram, y_ref, between=None):
    y_ref[...] = (gram[:, 0:128] + gram[:, 128:256]) * F32(0.5 ** 0.5)

    def sweep(step, carry):
        tall = y_ref[...]
        linv, = inverse_cholesky([dot(tall, tall, 0, 0)])
        ahead = jnp.where(step == SWEEPS - 1, tall, dot(gram[...], tall, 1, 0))
        y_ref[...] = dot(ahead, linv, 1, 1)
        if between is not None:
            between(step)
        return carry

    lax.fori_loop(0, SWEEPS, sweep, 0)
    return y_ref[...].astype(BF16)


def kernel(s_ref, basis_ref, energy_ref, rows_ref, part_ref, sum_ref, from_core, halves, from_plane, column,
           all_ref, diag_part, diag_core, diag_plane, diag_column, diag_sum, g_ref, g1_ref, y_ref, f_ref, d_ref, sent_ref, got_ref,
           own_sem, all_sem, diag_send, diag_recv, row_send, row_recv, sum_send, sum_recv, pair_send, pair_recv, out_send, out_recv):
    w = lax.axis_index("wide")
    y = lax.axis_index("narrow")
    core, x, z = lax.rem(w, 2), lax.rem(lax.div(w, 2), 4), lax.div(w, 8)
    n = rows_ref.shape[2]
    R = n * CHUNKS
    sibling = device(1 - core, x, y, z)
    plane = [(d, lax.rem(x + d // 4, 4), lax.rem(y + d % 4, 4)) for d in range(1, 16)]
    line = [(d, lax.rem(z + d, 8)) for d in range(1, 8)]

    barrier = pltpu.get_barrier_semaphore()
    peers = [device(core, x, y, pz) for d, pz in sorted(line, key=lambda v: abs(v[0] - 4))]
    peers += [device(core, px, py, z) for d, px, py in sorted(plane, key=lambda v: abs(v[0] // 4 - 2) + abs(v[0] % 4 - 2))]
    peers += [sibling]
    for peer in peers:
        pl.semaphore_signal(barrier, inc=1, device_id=peer, device_id_type=MESH)
    for c in range(CHUNKS):
        pltpu.make_async_copy(s_ref.at[at(y * R + c * n, n, 16)], rows_ref.at[c, y], own_sem).start()
    part_ref[...] = jnp.zeros_like(part_ref)
    pl.semaphore_wait(barrier, len(peers))

    for c in range(CHUNKS):
        for k in (2, 1, 3):
            py = lax.rem(y + k, 4)
            remote(s_ref.at[at(py * R + c * n, n, 16)], rows_ref.at[c, y], row_send, row_recv.at[c],
                   device(core, x, py, z)).start()
    whole = pltpu.make_async_copy(s_ref, all_ref, all_sem)
    whole.start()

    holds = core == lax.div(y, 2)
    diag_part[...] = jnp.zeros_like(diag_part)
    whole.wait()

    def tile(t, carry):
        value = all_ref[at(t * (4 * R // TILES), 4 * R // TILES, 16), :]
        diag_part[...] += dot(value, value, 0, 0, None)
        return carry

    lax.fori_loop(0, TILES, tile, 0)

    @pl.when(jnp.logical_not(holds))
    def _():
        remote(diag_part, diag_core, diag_send.at[0], diag_recv.at[0], sibling).start()

    @pl.when(holds)
    def _():
        arrived(diag_core, diag_recv.at[0])
        diag_part[...] += diag_core[...]
        for d in range(1, 4):
            px = lax.rem(x + d, 4)
            remote(diag_part.at[at(px * 32, 32)], diag_plane.at[d], diag_send.at[1], diag_recv.at[1],
                   device(core, px, y, z)).start()
        arrived(diag_plane.at[pl.ds(1, 3)], diag_recv.at[1])
        total = diag_part[at(x * 32, 32), :]
        for d in range(1, 4):
            total = total + diag_plane[d]
        diag_column[z] = total
        mine = diag_column.at[z]
        for d, pz in line:
            remote(mine, mine, diag_send.at[2], diag_recv.at[2], device(core, x, y, pz)).start()

    def diagonal_back():
        @pl.when(holds)
        def _():
            arrived(diag_column.at[pl.ds(0, 7)], diag_recv.at[2])
            total = diag_column[0]
            for k in range(1, 8):
                total = total + diag_column[k]
            mine = diag_sum.at[at(lax.rem(y, 2) * 128 + x * 32, 32)]
            mine[...] = total
            for d, px, py in plane:
                remote(mine, mine, diag_send.at[3], diag_recv.at[3], device(core, px, py, z)).start()

    def diagonal_there():
        @pl.when(holds)
        def _():
            arrived(diag_sum.at[pl.ds(0, 224)], diag_recv.at[3])

        @pl.when(jnp.logical_not(holds))
        def _():
            arrived(diag_sum, diag_recv.at[3])

    def diagonal_left():
        @pl.when(jnp.logical_not(holds))
        def _():
            arrived(diag_core, diag_send.at[0])

        @pl.when(holds)
        def _():
            arrived(diag_plane.at[pl.ds(1, 3)], diag_send.at[1])
            arrived(diag_column.at[pl.ds(0, 7)], diag_send.at[2])
            arrived(part_ref.at[pl.ds(0, 480)], diag_send.at[3])

    arrived(rows_ref.at[0], own_sem)
    for c in range(CHUNKS):
        arrived(rows_ref.at[c, pl.ds(0, 3)], row_recv.at[c])
        blocks = [rows_ref[c, j] for j in range(4)]
        for i in range(3):
            part = dot(blocks[i], jnp.concatenate(blocks[i + 1:], axis=1), 0, 0, None)
            for j in range(i + 1, 4):
                b = BLOCKS.index((i, j))
                part_ref[128 * b:128 * b + 128, :] += part[:, 128 * (j - i - 1):128 * (j - i)]

    q = x * 4 + y

    def sizes(p):
        start, length = PARTS[p]
        return start, length // 2, length // 32, start // 2

    def swap(p):
        start, half, piece, hs = sizes(p)
        remote(part_ref.at[at(start + (1 - core) * half, half)], from_core.at[pl.ds(hs, half)],
               sum_send.at[p, 0], sum_recv.at[p, 0], sibling).start()

    def after_swap(p):
        start, half, piece, hs = sizes(p)
        arrived(from_core.at[pl.ds(hs, half)], sum_recv.at[p, 0])
        halves[pl.ds(hs, half), :] = part_ref[at(start + core * half, half), :] + from_core[pl.ds(hs, half), :]
        for d, px, py in plane:
            remote(halves.at[at(hs + (px * 4 + py) * piece, piece)], from_plane.at[d, pl.ds(hs // 16, piece)],
                   sum_send.at[p, 1], sum_recv.at[p, 1], device(core, px, py, z)).start()

    def after_spread(p):
        start, half, piece, hs = sizes(p)
        arrived(from_plane.at[pl.ds(1, 15), pl.ds(hs // 16, piece)], sum_recv.at[p, 1])
        total = halves[at(hs + q * piece, piece), :]
        for d in range(1, 16):
            total = total + from_plane[d, pl.ds(hs // 16, piece), :]
        mine = column.at[z, pl.ds(hs // 16, piece)]
        mine[...] = total
        for d, pz in line:
            remote(mine, mine, sum_send.at[p, 2], sum_recv.at[p, 2], device(core, x, y, pz)).start()

    def after_ring(p):
        start, half, piece, hs = sizes(p)
        arrived(column.at[pl.ds(0, 7), pl.ds(hs // 16, piece)], sum_recv.at[p, 2])
        total = column[0, pl.ds(hs // 16, piece), :]
        for k in range(1, 8):
            total = total + column[k, pl.ds(hs // 16, piece), :]
        mine = sum_ref.at[at(start + core * half + q * piece, piece)]
        mine[...] = total
        for d, px, py in plane:
            remote(mine, mine, sum_send.at[p, 3], sum_recv.at[p, 3], device(core, px, py, z)).start()

    def after_back(p):
        start, half, piece, hs = sizes(p)
        arrived(sum_ref.at[pl.ds(start, 15 * piece)], sum_recv.at[p, 3])

    def last(p):
        start, half, piece, hs = sizes(p)
        mine = sum_ref.at[at(start + core * half, half)]
        remote(mine, mine, sum_send.at[p, 4], sum_recv.at[p, 4], sibling).start()

    def after_last(p):
        start, half, piece, hs = sizes(p)
        arrived(sum_ref.at[pl.ds(start, half)], sum_recv.at[p, 4])

    def all_left(p):
        start, half, piece, hs = sizes(p)
        arrived(from_core.at[pl.ds(hs, half)], sum_send.at[p, 0])
        arrived(from_plane.at[pl.ds(1, 15), pl.ds(hs // 16, piece)], sum_send.at[p, 1])
        arrived(column.at[pl.ds(0, 7), pl.ds(hs // 16, piece)], sum_send.at[p, 2])
        arrived(sum_ref.at[pl.ds(start, 15 * piece)], sum_send.at[p, 3])
        if p == 1:
            arrived(sum_ref.at[pl.ds(start, half)], sum_send.at[p, 4])

    swap(0)
    swap(1)
    after_swap(0)
    after_spread(0)
    diagonal_back()
    after_swap(1)
    after_ring(0)
    after_spread(1)
    diagonal_there()
    after_back(0)

    def between(step):
        @pl.when(step == 0)
        def _():
            after_ring(1)

        @pl.when(step == 1)
        def _():
            after_back(1)
            last(1)

    cross = sum_ref[at(core * 128, 128), :]
    g_ref[0:128, 0:128] = diag_sum[0:128, :]
    g_ref[0:128, 128:256] = cross
    g_ref[128:256, 0:128] = cross.T
    g_ref[128:256, 128:256] = diag_sum[128:256, :]
    own_factor = level(g_ref, y_ref, between)
    f_ref[core] = own_factor
    mine = f_ref.at[core]
    remote(mine, mine, pair_send.at[0], pair_recv.at[0], sibling).start()
    wide = own_factor.astype(F32)
    d_ref[core] = dot(wide, dot(g_ref[...], wide, 1, 0), 0, 0)
    block = d_ref.at[core]
    remote(block, block, pair_send.at[1], pair_recv.at[1], sibling).start()
    after_last(1)
    between_pairs = jnp.concatenate(
        [jnp.concatenate([sum_ref[256 + 256 * i + 128 * j:384 + 256 * i + 128 * j, :] for j in range(2)], axis=1)
         for i in range(2)], axis=0)
    arrived(f_ref.at[0], pair_recv.at[0])
    f0, f1 = f_ref[0], f_ref[1]
    cross = dot(f0.astype(F32), dot(between_pairs, f1.astype(F32), 1, 0), 0, 0)
    arrived(d_ref.at[0], pair_recv.at[1])
    g1_ref[0:128, 0:128] = d_ref[0]
    g1_ref[0:128, 128:256] = cross
    g1_ref[128:256, 0:128] = cross.T
    g1_ref[128:256, 128:256] = d_ref[1]
    f = level(g1_ref, y_ref)
    weights = jnp.concatenate([dot(f[0:128], f0, 0, 1, None), dot(f[128:256], f1, 0, 1, None)], axis=1).astype(BF16)
    wide = f.astype(F32)
    squares = dot(wide, dot(g1_ref[...], wide, 1, 0), 0, 0)
    diagonal = lax.broadcasted_iota(jnp.int32, (128, 128), 0) == lax.broadcasted_iota(jnp.int32, (128, 128), 1)
    squares = jnp.where(diagonal, squares, 0.0)
    inverse = 1.0 / jnp.sqrt(jnp.sum(squares, axis=1, keepdims=True) + EPSILON)
    energies = jnp.sqrt(jnp.sum(squares, axis=0, keepdims=True) + EPSILON)
    share = jnp.zeros((1, 32), F32)
    for j in range(4):
        share = jnp.where(y == j, energies[:, 32 * j:32 * j + 32], share)
    energy_ref[...] = share

    for c in range(CHUNKS):
        block = jnp.concatenate([rows_ref[c, j] for j in range(4)], axis=1)
        part = (dot(weights, block, 1, 1, None) * inverse).astype(BF16)
        for j in range(4):
            sent_ref[c, j] = part[32 * j:32 * j + 32, :]
        for k in (2, 1, 3):
            py = lax.rem(y + k, 4)
            remote(sent_ref.at[c, py], got_ref.at[c, y], out_send, out_recv.at[c], device(core, x, py, z)).start()
    for c in range(CHUNKS):
        basis_ref[:, at(y * R + c * n, n, 128)] = sent_ref[c, y].astype(F32)
    for c in range(CHUNKS):
        arrived(got_ref.at[c, pl.ds(0, 3)], out_recv.at[c])
        for k in (1, 2, 3):
            py = lax.rem(y + k, 4)
            basis_ref[:, at(py * R + c * n, n, 128)] = got_ref[c, py].astype(F32)
    arrived(rows_ref.at[pl.ds(0, 3)], row_send)
    diagonal_left()
    for p in range(len(PARTS)):
        all_left(p)
    arrived(f_ref.at[0], pair_send.at[0])
    arrived(d_ref.at[0], pair_send.at[1])
    arrived(got_ref.at[pl.ds(0, 3)], out_send)


def body(snapshots):
    R = snapshots.shape[0] // 4
    total = sum(length for _, length in PARTS)
    basis, energies = pl.pallas_call(
        kernel,
        out_shape=(jax.ShapeDtypeStruct((32, 4 * R), F32), jax.ShapeDtypeStruct((1, 32), F32)),
        in_specs=[pl.BlockSpec(memory_space=pl.ANY)],
        out_specs=(pl.BlockSpec(memory_space=pltpu.VMEM),) * 2,
        scratch_shapes=[
            pltpu.VMEM((CHUNKS, 4, R // CHUNKS, 128), BF16),
            pltpu.VMEM((total, 128), F32),
            pltpu.VMEM((total, 128), F32),
            pltpu.VMEM((total // 2, 128), F32),
            pltpu.VMEM((total // 2, 128), F32),
            pltpu.VMEM((16, total // 32, 128), F32),
            pltpu.VMEM((8, total // 32, 128), F32),
            pltpu.VMEM((4 * R, 128), BF16),
            pltpu.VMEM((128, 128), F32),
            pltpu.VMEM((128, 128), F32),
            pltpu.VMEM((4, 32, 128), F32),
            pltpu.VMEM((8, 32, 128), F32),
            pltpu.VMEM((256, 128), F32),
            pltpu.VMEM((256, 256), F32),
            pltpu.VMEM((256, 256), F32),
            pltpu.VMEM((256, 128), F32),
            pltpu.VMEM((2, 256, 128), BF16),
            pltpu.VMEM((2, 128, 128), F32),
            pltpu.VMEM((CHUNKS, 4, 32, R // CHUNKS), BF16),
            pltpu.VMEM((CHUNKS, 4, 32, R // CHUNKS), BF16),
            pltpu.SemaphoreType.DMA,
            pltpu.SemaphoreType.DMA,
            pltpu.SemaphoreType.DMA((4,)),
            pltpu.SemaphoreType.DMA((4,)),
            pltpu.SemaphoreType.DMA,
            pltpu.SemaphoreType.DMA((CHUNKS,)),
            pltpu.SemaphoreType.DMA((2, 5)),
            pltpu.SemaphoreType.DMA((2, 5)),
            pltpu.SemaphoreType.DMA((2,)),
            pltpu.SemaphoreType.DMA((2,)),
            pltpu.SemaphoreType.DMA,
            pltpu.SemaphoreType.DMA((CHUNKS,)),
        ],
        compiler_params=pltpu.CompilerParams(collective_id=0, has_side_effects=True, vmem_limit_bytes=103 * 512 * 1024),
    )(snapshots)
    return basis.T, energies.reshape(32)


def solution(mesh):
    return jax.shard_map(body, mesh=mesh, in_specs=(P("wide", "narrow"),), out_specs=(P("wide", "narrow"), P("narrow")),
                         check_vma=False)
```

```python
import functools

import jax
import jax.numpy as jnp
from jax import lax
from jax.experimental import pallas as pl
from jax.experimental.pallas import tpu as pltpu
from jax.sharding import PartitionSpec as P

MESH = pl.DeviceIdType.MESH
HI = lax.Precision.HIGHEST
F32 = jnp.float32
BF16 = jnp.bfloat16
SWEEPS = 3
EPSILON = 1e-6
BLOCKS = ((0, 1), (2, 3), (0, 2), (0, 3), (1, 2), (1, 3))
PARTS = ((0, 256), (256, 512))
TILES = 8
CHUNKS = 4


def dot(a, b, ca, cb, precision=HI):
    return lax.dot_general(a, b, (((ca,), (cb,)), ((), ())), precision=precision, preferred_element_type=F32)


def thirds(a):
    high = a.astype(BF16)
    rest = a - high.astype(F32)
    middle = rest.astype(BF16)
    return high, middle, (rest - middle.astype(F32)).astype(BF16)


def short_dot(a, b):
    ah, am, al = thirds(a)
    bh, bm, bl = thirds(b)
    left = jnp.concatenate([ah, ah, am, am, ah, al], axis=0)
    right = jnp.concatenate([bh, bm, bh, bm, bl, bh], axis=0)
    return lax.dot_general(left, right, (((0,), (0,)), ((), ())), preferred_element_type=F32)


def inverse_cholesky(mats, outer=4, wide=2):
    n = 128
    lane = lax.broadcasted_iota(jnp.int32, (8, n), 1)
    sub = lax.broadcasted_iota(jnp.int32, (8, n), 0)
    S = [[a[8 * r:8 * r + 8, :] for r in range(n // 8)] for a in mats]
    M = range(len(mats))
    inverse_pivots = [[] for m in M]
    full = lambda row: jnp.broadcast_to(row, (8, n))
    for first in range(0, n // 8, outer):
        last = first + outer
        for p in range(first, last, wide):
            base = 8 * p
            inblock = (lane >= base) & (lane < base + 8 * wide)
            E = [[{r: full(S[m][r][:, base + j:base + j + 1]) for r in range(p + j // 8, last)}
                  for j in range(8 * wide)] for m in M]
            for m in M:
                for r in range(p, last):
                    fill = jnp.where(lane - 8 * r == sub, 1.0, 0.0) if r < p + wide else 0.0
                    S[m][r] = jnp.where(inblock, fill, S[m][r])
            scale = [[jnp.zeros((8, n), F32)] * wide for m in M]
            for k in range(8 * wide):
                top, row = p + k // 8, k % 8
                inv = [1.0 / full(E[m][k][top][row:row + 1, :]) for m in M]
                for m in M:
                    scale[m][k // 8] = jnp.where(sub == row, inv[m], scale[m][k // 8])
                    pivots = {j: full(E[m][k][p + j // 8][j % 8:j % 8 + 1, :]) for j in range(k + 1, 8 * wide)}
                    pivot_row = full(S[m][top][row:row + 1, :])
                    for r in range(top, last):
                        mult = E[m][k][r] * inv[m]
                        if r == top:
                            mult = jnp.where(sub > row, mult, 0.0)
                        for j in range(k + 1, 8 * wide):
                            if r >= p + j // 8:
                                E[m][j][r] = E[m][j][r] - mult * pivots[j]
                        S[m][r] = S[m][r] - mult * pivot_row
            for m in M:
                inverse_pivots[m] += scale[m]
        if last < n // 8:
            for m in M:
                left = jnp.concatenate([jnp.where(lane >= 8 * last, S[m][p] * inverse_pivots[m][p], 0.0)
                                        for p in range(first, last)], axis=0)
                right = jnp.concatenate(
                    [jnp.where((lane >= 8 * last) | (lane < 8 * (p - (p - first) % wide + wide)), S[m][p], 0.0)
                     for p in range(first, last)], axis=0)
                update = short_dot(left, right)
                outside = (lane < 8 * first) | (lane >= 8 * last)
                for r in range(last, n // 8):
                    S[m][r] = jnp.where(outside, S[m][r], 0.0) - update[8 * r:8 * r + 8, :]
    return [jnp.concatenate([jnp.where(lane <= sub + 8 * r, S[m][r] * jnp.sqrt(inverse_pivots[m][r]), 0.0) for r in range(n // 8)], axis=0) for m in M]


def right_factor(a, f):
    return lax.dot_general(jnp.concatenate(thirds(a), axis=1), jnp.concatenate([f, f, f], axis=0),
                           (((1,), (0,)), ((), ())), preferred_element_type=F32)


def left_factor(f, a):
    return lax.dot_general(jnp.concatenate([f, f, f], axis=0), jnp.concatenate(thirds(a), axis=0),
                           (((0,), (0,)), ((), ())), preferred_element_type=F32)


def device(core, x, y, z):
    return {"wide": (z * 4 + x) * 2 + core, "narrow": y}


def remote(src, dst, send, recv, peer):
    return pltpu.make_async_remote_copy(src_ref=src, dst_ref=dst, send_sem=send, recv_sem=recv,
                                        device_id=peer, device_id_type=MESH)


def at(start, size, align=8):
    return pl.ds(pl.multiple_of(start, align), size)


def start_all(copies):
    for copy in copies:
        copy.start()


def arrived(like, sem):
    pltpu.make_async_copy(like, like, sem).wait()


def level(gram, y_ref, between=None):
    y_ref[...] = (gram[:, 0:128] + gram[:, 128:256]) * F32(0.5 ** 0.5)

    def sweep(step, carry):
        tall = y_ref[...]
        linv, = inverse_cholesky([dot(tall, tall, 0, 0)])
        ahead = jnp.where(step == SWEEPS - 1, tall, dot(gram[...], tall, 1, 0))
        y_ref[...] = dot(ahead, linv, 1, 1)
        if between is not None:
            between(step)
        return carry

    lax.fori_loop(0, SWEEPS, sweep, 0)
    return y_ref[...].astype(BF16)


def kernel(s_ref, basis_ref, energy_ref, rows_ref, part_ref, sum_ref, from_core, halves, from_plane, column,
           all_ref, diag_part, diag_core, diag_plane, diag_column, diag_sum, g_ref, g1_ref, y_ref, f_ref, d_ref, sent_ref, got_ref,
           own_sem, all_sem, diag_send, diag_recv, row_send, row_recv, sum_send, sum_recv, pair_send, pair_recv, out_send, out_recv):
    w = lax.axis_index("wide")
    y = lax.axis_index("narrow")
    core, x, z = lax.rem(w, 2), lax.rem(lax.div(w, 2), 4), lax.div(w, 8)
    n = rows_ref.shape[2]
    R = n * CHUNKS
    sibling = device(1 - core, x, y, z)
    plane = [(d, lax.rem(x + d // 4, 4), lax.rem(y + d % 4, 4)) for d in range(1, 16)]
    line = [(d, lax.rem(z + d, 8)) for d in range(1, 8)]

    barrier = pltpu.get_barrier_semaphore()
    peers = [device(core, x, y, pz) for d, pz in sorted(line, key=lambda v: abs(v[0] - 4))]
    peers += [device(core, px, py, z) for d, px, py in sorted(plane, key=lambda v: abs(v[0] // 4 - 2) + abs(v[0] % 4 - 2))]
    peers += [sibling]
    for peer in peers:
        pl.semaphore_signal(barrier, inc=1, device_id=peer, device_id_type=MESH)
    for c in range(CHUNKS):
        pltpu.make_async_copy(s_ref.at[at(y * R + c * n, n, 16)], rows_ref.at[c, y], own_sem).start()
    part_ref[...] = jnp.zeros_like(part_ref)
    pl.semaphore_wait(barrier, len(peers))

    for c in range(CHUNKS):
        for k in (2, 1, 3):
            py = lax.rem(y + k, 4)
            remote(s_ref.at[at(py * R + c * n, n, 16)], rows_ref.at[c, y], row_send, row_recv.at[c],
                   device(core, x, py, z)).start()
    whole = pltpu.make_async_copy(s_ref, all_ref, all_sem)
    whole.start()

    holds = core == lax.div(y, 2)
    diag_part[...] = jnp.zeros_like(diag_part)
    whole.wait()

    def tile(t, carry):
        value = all_ref[at(t * (4 * R // TILES), 4 * R // TILES, 16), :]
        diag_part[...] += dot(value, value, 0, 0, None)
        return carry

    lax.fori_loop(0, TILES, tile, 0)

    @pl.when(jnp.logical_not(holds))
    def _():
        remote(diag_part, diag_core, diag_send.at[0], diag_recv.at[0], sibling).start()

    @pl.when(holds)
    def _():
        arrived(diag_core, diag_recv.at[0])
        diag_part[...] += diag_core[...]
        for d in range(1, 4):
            px = lax.rem(x + d, 4)
            remote(diag_part.at[at(px * 32, 32)], diag_plane.at[d], diag_send.at[1], diag_recv.at[1],
                   device(core, px, y, z)).start()
        arrived(diag_plane.at[pl.ds(1, 3)], diag_recv.at[1])
        total = diag_part[at(x * 32, 32), :]
        for d in range(1, 4):
            total = total + diag_plane[d]
        diag_column[z] = total
        mine = diag_column.at[z]
        for d, pz in line:
            remote(mine, mine, diag_send.at[2], diag_recv.at[2], device(core, x, y, pz)).start()

    def diagonal_back():
        @pl.when(holds)
        def _():
            arrived(diag_column.at[pl.ds(0, 7)], diag_recv.at[2])
            total = diag_column[0]
            for k in range(1, 8):
                total = total + diag_column[k]
            mine = diag_sum.at[at(lax.rem(y, 2) * 128 + x * 32, 32)]
            mine[...] = total
            for d, px, py in plane:
                remote(mine, mine, diag_send.at[3], diag_recv.at[3], device(core, px, py, z)).start()

    def diagonal_there():
        @pl.when(holds)
        def _():
            arrived(diag_sum.at[pl.ds(0, 224)], diag_recv.at[3])

        @pl.when(jnp.logical_not(holds))
        def _():
            arrived(diag_sum, diag_recv.at[3])

    def diagonal_left():
        @pl.when(jnp.logical_not(holds))
        def _():
            arrived(diag_core, diag_send.at[0])

        @pl.when(holds)
        def _():
            arrived(diag_plane.at[pl.ds(1, 3)], diag_send.at[1])
            arrived(diag_column.at[pl.ds(0, 7)], diag_send.at[2])
            arrived(part_ref.at[pl.ds(0, 480)], diag_send.at[3])

    arrived(rows_ref.at[pl.ds(0, CHUNKS // 4)], own_sem)
    for c in range(CHUNKS):
        arrived(rows_ref.at[c, pl.ds(0, 3)], row_recv.at[c])
        blocks = [rows_ref[c, j] for j in range(4)]
        for i in range(3):
            part = dot(blocks[i], jnp.concatenate(blocks[i + 1:], axis=1), 0, 0, None)
            for j in range(i + 1, 4):
                b = BLOCKS.index((i, j))
                part_ref[128 * b:128 * b + 128, :] += part[:, 128 * (j - i - 1):128 * (j - i)]

    q = x * 4 + y

    def sizes(p):
        start, length = PARTS[p]
        return start, length // 2, length // 32, start // 2

    def swap(p):
        start, half, piece, hs = sizes(p)
        remote(part_ref.at[at(start + (1 - core) * half, half)], from_core.at[pl.ds(hs, half)],
               sum_send.at[p, 0], sum_recv.at[p, 0], sibling).start()

    def after_swap(p):
        start, half, piece, hs = sizes(p)
        arrived(from_core.at[pl.ds(hs, half)], sum_recv.at[p, 0])
        halves[pl.ds(hs, half), :] = part_ref[at(start + core * half, half), :] + from_core[pl.ds(hs, half), :]
        for d, px, py in plane:
            remote(halves.at[at(hs + (px * 4 + py) * piece, piece)], from_plane.at[d, pl.ds(hs // 16, piece)],
                   sum_send.at[p, 1], sum_recv.at[p, 1], device(core, px, py, z)).start()

    def after_spread(p):
        start, half, piece, hs = sizes(p)
        arrived(from_plane.at[pl.ds(1, 15), pl.ds(hs // 16, piece)], sum_recv.at[p, 1])
        total = halves[at(hs + q * piece, piece), :]
        for d in range(1, 16):
            total = total + from_plane[d, pl.ds(hs // 16, piece), :]
        mine = column.at[z, pl.ds(hs // 16, piece)]
        mine[...] = total
        for d, pz in line:
            remote(mine, mine, sum_send.at[p, 2], sum_recv.at[p, 2], device(core, x, y, pz)).start()

    def after_ring(p):
        start, half, piece, hs = sizes(p)
        arrived(column.at[pl.ds(0, 7), pl.ds(hs // 16, piece)], sum_recv.at[p, 2])
        total = column[0, pl.ds(hs // 16, piece), :]
        for k in range(1, 8):
            total = total + column[k, pl.ds(hs // 16, piece), :]
        mine = sum_ref.at[at(start + core * half + q * piece, piece)]
        mine[...] = total
        for d, px, py in plane:
            remote(mine, mine, sum_send.at[p, 3], sum_recv.at[p, 3], device(core, px, py, z)).start()

    def after_back(p):
        start, half, piece, hs = sizes(p)
        arrived(sum_ref.at[pl.ds(start, 15 * piece)], sum_recv.at[p, 3])

    def last(p):
        start, half, piece, hs = sizes(p)
        mine = sum_ref.at[at(start + core * half, half)]
        remote(mine, mine, sum_send.at[p, 4], sum_recv.at[p, 4], sibling).start()

    def after_last(p):
        start, half, piece, hs = sizes(p)
        arrived(sum_ref.at[pl.ds(start, half)], sum_recv.at[p, 4])

    def all_left(p):
        start, half, piece, hs = sizes(p)
        arrived(from_core.at[pl.ds(hs, half)], sum_send.at[p, 0])
        arrived(from_plane.at[pl.ds(1, 15), pl.ds(hs // 16, piece)], sum_send.at[p, 1])
        arrived(column.at[pl.ds(0, 7), pl.ds(hs // 16, piece)], sum_send.at[p, 2])
        arrived(sum_ref.at[pl.ds(start, 15 * piece)], sum_send.at[p, 3])
        if p == 1:
            arrived(sum_ref.at[pl.ds(start, half)], sum_send.at[p, 4])

    swap(0)
    swap(1)
    after_swap(0)
    after_spread(0)
    diagonal_back()
    after_swap(1)
    after_ring(0)
    after_spread(1)
    diagonal_there()
    after_back(0)

    def between(step):
        @pl.when(step == 0)
        def _():
            after_ring(1)

    cross = sum_ref[at(core * 128, 128), :]
    g_ref[0:128, 0:128] = diag_sum[0:128, :]
    g_ref[0:128, 128:256] = cross
    g_ref[128:256, 0:128] = cross.T
    g_ref[128:256, 128:256] = diag_sum[128:256, :]
    own_factor = level(g_ref, y_ref, between)
    f_ref[core] = own_factor
    mine = f_ref.at[core]
    remote(mine, mine, pair_send.at[0], pair_recv.at[0], sibling).start()
    after_back(1)
    last(1)
    d_ref[core] = left_factor(own_factor, right_factor(g_ref[...], own_factor))
    block = d_ref.at[core]
    remote(block, block, pair_send.at[1], pair_recv.at[1], sibling).start()
    after_last(1)
    between_pairs = jnp.concatenate(
        [jnp.concatenate([sum_ref[256 + 256 * i + 128 * j:384 + 256 * i + 128 * j, :] for j in range(2)], axis=1)
         for i in range(2)], axis=0)
    arrived(f_ref.at[0], pair_recv.at[0])
    f0, f1 = f_ref[0], f_ref[1]
    cross = left_factor(f0, right_factor(between_pairs, f1))
    arrived(d_ref.at[0], pair_recv.at[1])
    g1_ref[0:128, 0:128] = d_ref[0]
    g1_ref[0:128, 128:256] = cross
    g1_ref[128:256, 0:128] = cross.T
    g1_ref[128:256, 128:256] = d_ref[1]
    f = level(g1_ref, y_ref)
    weights = jnp.concatenate([dot(f[0:128], f0, 0, 1, None), dot(f[128:256], f1, 0, 1, None)], axis=1).astype(BF16)
    squares = left_factor(f, right_factor(g1_ref[...], f))
    diagonal = lax.broadcasted_iota(jnp.int32, (128, 128), 0) == lax.broadcasted_iota(jnp.int32, (128, 128), 1)
    squares = jnp.where(diagonal, squares, 0.0)
    inverse = 1.0 / jnp.sqrt(jnp.sum(squares, axis=1, keepdims=True) + EPSILON)
    energies = jnp.sqrt(jnp.sum(squares, axis=0, keepdims=True) + EPSILON)
    share = jnp.zeros((1, 32), F32)
    for j in range(4):
        share = jnp.where(y == j, energies[:, 32 * j:32 * j + 32], share)
    energy_ref[...] = share

    for c in range(CHUNKS):
        block = jnp.concatenate([rows_ref[c, j] for j in range(4)], axis=1)
        part = (dot(weights, block, 1, 1, None) * inverse).astype(BF16)
        for j in range(4):
            sent_ref[c, j] = part[32 * j:32 * j + 32, :]
        for k in (2, 1, 3):
            py = lax.rem(y + k, 4)
            remote(sent_ref.at[c, py], got_ref.at[c, y], out_send, out_recv.at[c], device(core, x, py, z)).start()
    for c in range(CHUNKS):
        basis_ref[:, at(y * R + c * n, n, 128)] = sent_ref[c, y].astype(F32)
    for c in range(CHUNKS):
        arrived(got_ref.at[c, pl.ds(0, 3)], out_recv.at[c])
        for k in (1, 2, 3):
            py = lax.rem(y + k, 4)
            basis_ref[:, at(py * R + c * n, n, 128)] = got_ref[c, py].astype(F32)
    arrived(rows_ref.at[pl.ds(0, 3 * CHUNKS // 4)], row_send)
    diagonal_left()
    for p in range(len(PARTS)):
        all_left(p)
    arrived(f_ref.at[0], pair_send.at[0])
    arrived(d_ref.at[0], pair_send.at[1])
    arrived(got_ref.at[pl.ds(0, 3 * CHUNKS // 4)], out_send)


def body(snapshots):
    R = snapshots.shape[0] // 4
    total = sum(length for _, length in PARTS)
    basis, energies = pl.pallas_call(
        kernel,
        out_shape=(jax.ShapeDtypeStruct((32, 4 * R), F32), jax.ShapeDtypeStruct((1, 32), F32)),
        in_specs=[pl.BlockSpec(memory_space=pl.ANY)],
        out_specs=(pl.BlockSpec(memory_space=pltpu.VMEM),) * 2,
        scratch_shapes=[
            pltpu.VMEM((CHUNKS, 4, R // CHUNKS, 128), BF16),
            pltpu.VMEM((total, 128), F32),
            pltpu.VMEM((total, 128), F32),
            pltpu.VMEM((total // 2, 128), F32),
            pltpu.VMEM((total // 2, 128), F32),
            pltpu.VMEM((16, total // 32, 128), F32),
            pltpu.VMEM((8, total // 32, 128), F32),
            pltpu.VMEM((4 * R, 128), BF16),
            pltpu.VMEM((128, 128), F32),
            pltpu.VMEM((128, 128), F32),
            pltpu.VMEM((4, 32, 128), F32),
            pltpu.VMEM((8, 32, 128), F32),
            pltpu.VMEM((256, 128), F32),
            pltpu.VMEM((256, 256), F32),
            pltpu.VMEM((256, 256), F32),
            pltpu.VMEM((256, 128), F32),
            pltpu.VMEM((2, 256, 128), BF16),
            pltpu.VMEM((2, 128, 128), F32),
            pltpu.VMEM((CHUNKS, 4, 32, R // CHUNKS), BF16),
            pltpu.VMEM((CHUNKS, 4, 32, R // CHUNKS), BF16),
            pltpu.SemaphoreType.DMA,
            pltpu.SemaphoreType.DMA,
            pltpu.SemaphoreType.DMA((4,)),
            pltpu.SemaphoreType.DMA((4,)),
            pltpu.SemaphoreType.DMA,
            pltpu.SemaphoreType.DMA((CHUNKS,)),
            pltpu.SemaphoreType.DMA((2, 5)),
            pltpu.SemaphoreType.DMA((2, 5)),
            pltpu.SemaphoreType.DMA((2,)),
            pltpu.SemaphoreType.DMA((2,)),
            pltpu.SemaphoreType.DMA,
            pltpu.SemaphoreType.DMA((CHUNKS,)),
        ],
        compiler_params=pltpu.CompilerParams(collective_id=0, has_side_effects=True, vmem_limit_bytes=103 * 512 * 1024),
    )(snapshots)
    return basis.T, energies.reshape(32)


def solution(mesh):
    return jax.shard_map(body, mesh=mesh, in_specs=(P("wide", "narrow"),), out_specs=(P("wide", "narrow"), P("narrow")),
                         check_vma=False)
```

```python
import functools

import jax
import jax.numpy as jnp
from jax import lax
from jax.experimental import pallas as pl
from jax.experimental.pallas import tpu as pltpu
from jax.sharding import PartitionSpec as P

MESH = pl.DeviceIdType.MESH
HI = lax.Precision.HIGHEST
F32 = jnp.float32
BF16 = jnp.bfloat16
SWEEPS = 3
EPSILON = 1e-6
BLOCKS = ((0, 1), (2, 3), (0, 2), (0, 3), (1, 2), (1, 3))
PARTS = ((0, 256), (256, 512))
TILES = 8
CHUNKS = 8


def dot(a, b, ca, cb, precision=HI):
    return lax.dot_general(a, b, (((ca,), (cb,)), ((), ())), precision=precision, preferred_element_type=F32)


def thirds(a):
    high = a.astype(BF16)
    rest = a - high.astype(F32)
    middle = rest.astype(BF16)
    return high, middle, (rest - middle.astype(F32)).astype(BF16)


def short_dot(a, b):
    ah, am, al = thirds(a)
    bh, bm, bl = thirds(b)
    left = jnp.concatenate([ah, ah, am, am, ah, al], axis=0)
    right = jnp.concatenate([bh, bm, bh, bm, bl, bh], axis=0)
    return lax.dot_general(left, right, (((0,), (0,)), ((), ())), preferred_element_type=F32)


def inverse_cholesky(mats, outer=4, wide=2):
    n = 128
    lane = lax.broadcasted_iota(jnp.int32, (8, n), 1)
    sub = lax.broadcasted_iota(jnp.int32, (8, n), 0)
    S = [[a[8 * r:8 * r + 8, :] for r in range(n // 8)] for a in mats]
    M = range(len(mats))
    inverse_pivots = [[] for m in M]
    full = lambda row: jnp.broadcast_to(row, (8, n))
    for first in range(0, n // 8, outer):
        last = first + outer
        for p in range(first, last, wide):
            base = 8 * p
            inblock = (lane >= base) & (lane < base + 8 * wide)
            E = [[{r: full(S[m][r][:, base + j:base + j + 1]) for r in range(p + j // 8, last)}
                  for j in range(8 * wide)] for m in M]
            for m in M:
                for r in range(p, last):
                    fill = jnp.where(lane - 8 * r == sub, 1.0, 0.0) if r < p + wide else 0.0
                    S[m][r] = jnp.where(inblock, fill, S[m][r])
            scale = [[jnp.zeros((8, n), F32)] * wide for m in M]
            for k in range(8 * wide):
                top, row = p + k // 8, k % 8
                inv = [1.0 / full(E[m][k][top][row:row + 1, :]) for m in M]
                for m in M:
                    scale[m][k // 8] = jnp.where(sub == row, inv[m], scale[m][k // 8])
                    pivots = {j: full(E[m][k][p + j // 8][j % 8:j % 8 + 1, :]) for j in range(k + 1, 8 * wide)}
                    pivot_row = full(S[m][top][row:row + 1, :])
                    for r in range(top, last):
                        mult = E[m][k][r] * inv[m]
                        if r == top:
                            mult = jnp.where(sub > row, mult, 0.0)
                        for j in range(k + 1, 8 * wide):
                            if r >= p + j // 8:
                                E[m][j][r] = E[m][j][r] - mult * pivots[j]
                        S[m][r] = S[m][r] - mult * pivot_row
            for m in M:
                inverse_pivots[m] += scale[m]
        if last < n // 8:
            for m in M:
                left = jnp.concatenate([jnp.where(lane >= 8 * last, S[m][p] * inverse_pivots[m][p], 0.0)
                                        for p in range(first, last)], axis=0)
                right = jnp.concatenate(
                    [jnp.where((lane >= 8 * last) | (lane < 8 * (p - (p - first) % wide + wide)), S[m][p], 0.0)
                     for p in range(first, last)], axis=0)
                update = short_dot(left, right)
                outside = (lane < 8 * first) | (lane >= 8 * last)
                for r in range(last, n // 8):
                    S[m][r] = jnp.where(outside, S[m][r], 0.0) - update[8 * r:8 * r + 8, :]
    return [jnp.concatenate([jnp.where(lane <= sub + 8 * r, S[m][r] * jnp.sqrt(inverse_pivots[m][r]), 0.0) for r in range(n // 8)], axis=0) for m in M]


def right_factor(a, f):
    return lax.dot_general(jnp.concatenate(thirds(a), axis=1), jnp.concatenate([f, f, f], axis=0),
                           (((1,), (0,)), ((), ())), preferred_element_type=F32)


def left_factor(f, a):
    return lax.dot_general(jnp.concatenate([f, f, f], axis=0), jnp.concatenate(thirds(a), axis=0),
                           (((0,), (0,)), ((), ())), preferred_element_type=F32)


def device(core, x, y, z):
    return {"wide": (z * 4 + x) * 2 + core, "narrow": y}


def remote(src, dst, send, recv, peer):
    return pltpu.make_async_remote_copy(src_ref=src, dst_ref=dst, send_sem=send, recv_sem=recv,
                                        device_id=peer, device_id_type=MESH)


def at(start, size, align=8):
    return pl.ds(pl.multiple_of(start, align), size)


def start_all(copies):
    for copy in copies:
        copy.start()


def arrived(like, sem):
    pltpu.make_async_copy(like, like, sem).wait()


def level(gram, y_ref, between=None):
    y_ref[...] = (gram[:, 0:128] + gram[:, 128:256]) * F32(0.5 ** 0.5)

    def sweep(step, carry):
        tall = y_ref[...]
        linv, = inverse_cholesky([dot(tall, tall, 0, 0)])
        ahead = jnp.where(step == SWEEPS - 1, tall, dot(gram[...], tall, 1, 0))
        y_ref[...] = dot(ahead, linv, 1, 1)
        if between is not None:
            between(step)
        return carry

    lax.fori_loop(0, SWEEPS, sweep, 0)
    return y_ref[...].astype(BF16)


def kernel(s_ref, basis_ref, energy_ref, rows_ref, part_ref, sum_ref, from_core, halves, from_plane, column,
           all_ref, diag_part, diag_core, diag_plane, diag_column, diag_sum, g_ref, g1_ref, y_ref, f_ref, d_ref, sent_ref, got_ref,
           own_sem, all_sem, diag_send, diag_recv, row_send, row_recv, sum_send, sum_recv, pair_send, pair_recv, out_send, out_recv):
    w = lax.axis_index("wide")
    y = lax.axis_index("narrow")
    core, x, z = lax.rem(w, 2), lax.rem(lax.div(w, 2), 4), lax.div(w, 8)
    n = rows_ref.shape[2]
    R = n * CHUNKS
    sibling = device(1 - core, x, y, z)
    plane = [(d, lax.rem(x + d // 4, 4), lax.rem(y + d % 4, 4)) for d in range(1, 16)]
    line = [(d, lax.rem(z + d, 8)) for d in range(1, 8)]

    barrier = pltpu.get_barrier_semaphore()
    peers = [device(core, x, y, pz) for d, pz in sorted(line, key=lambda v: abs(v[0] - 4))]
    peers += [device(core, px, py, z) for d, px, py in sorted(plane, key=lambda v: abs(v[0] // 4 - 2) + abs(v[0] % 4 - 2))]
    peers += [sibling]
    for peer in peers:
        pl.semaphore_signal(barrier, inc=1, device_id=peer, device_id_type=MESH)
    for c in range(CHUNKS):
        pltpu.make_async_copy(s_ref.at[at(y * R + c * n, n, 16)], rows_ref.at[c, y], own_sem).start()
    part_ref[...] = jnp.zeros_like(part_ref)
    pl.semaphore_wait(barrier, len(peers))

    for c in range(CHUNKS):
        for k in (2, 1, 3):
            py = lax.rem(y + k, 4)
            remote(s_ref.at[at(py * R + c * n, n, 16)], rows_ref.at[c, y], row_send, row_recv.at[c],
                   device(core, x, py, z)).start()
    whole = pltpu.make_async_copy(s_ref, all_ref, all_sem)
    whole.start()

    holds = core == lax.div(y, 2)
    diag_part[...] = jnp.zeros_like(diag_part)
    whole.wait()

    def tile(t, carry):
        value = all_ref[at(t * (4 * R // TILES), 4 * R // TILES, 16), :]
        diag_part[...] += dot(value, value, 0, 0, None)
        return carry

    lax.fori_loop(0, TILES, tile, 0)

    @pl.when(jnp.logical_not(holds))
    def _():
        remote(diag_part, diag_core, diag_send.at[0], diag_recv.at[0], sibling).start()

    @pl.when(holds)
    def _():
        arrived(diag_core, diag_recv.at[0])
        diag_part[...] += diag_core[...]
        for d in range(1, 4):
            px = lax.rem(x + d, 4)
            remote(diag_part.at[at(px * 32, 32)], diag_plane.at[d], diag_send.at[1], diag_recv.at[1],
                   device(core, px, y, z)).start()
        arrived(diag_plane.at[pl.ds(1, 3)], diag_recv.at[1])
        total = diag_part[at(x * 32, 32), :]
        for d in range(1, 4):
            total = total + diag_plane[d]
        diag_column[z] = total
        mine = diag_column.at[z]
        for d, pz in line:
            remote(mine, mine, diag_send.at[2], diag_recv.at[2], device(core, x, y, pz)).start()

    def diagonal_back():
        @pl.when(holds)
        def _():
            arrived(diag_column.at[pl.ds(0, 7)], diag_recv.at[2])
            total = diag_column[0]
            for k in range(1, 8):
                total = total + diag_column[k]
            mine = diag_sum.at[at(lax.rem(y, 2) * 128 + x * 32, 32)]
            mine[...] = total
            for d, px, py in plane:
                remote(mine, mine, diag_send.at[3], diag_recv.at[3], device(core, px, py, z)).start()

    def diagonal_there():
        @pl.when(holds)
        def _():
            arrived(diag_sum.at[pl.ds(0, 224)], diag_recv.at[3])

        @pl.when(jnp.logical_not(holds))
        def _():
            arrived(diag_sum, diag_recv.at[3])

    def diagonal_left():
        @pl.when(jnp.logical_not(holds))
        def _():
            arrived(diag_core, diag_send.at[0])

        @pl.when(holds)
        def _():
            arrived(diag_plane.at[pl.ds(1, 3)], diag_send.at[1])
            arrived(diag_column.at[pl.ds(0, 7)], diag_send.at[2])
            arrived(part_ref.at[pl.ds(0, 480)], diag_send.at[3])

    arrived(rows_ref.at[pl.ds(0, CHUNKS // 4)], own_sem)
    for c in range(CHUNKS):
        arrived(rows_ref.at[c, pl.ds(0, 3)], row_recv.at[c])
        blocks = [rows_ref[c, j] for j in range(4)]
        for i in range(3):
            part = dot(blocks[i], jnp.concatenate(blocks[i + 1:], axis=1), 0, 0, None)
            for j in range(i + 1, 4):
                b = BLOCKS.index((i, j))
                part_ref[128 * b:128 * b + 128, :] += part[:, 128 * (j - i - 1):128 * (j - i)]

    q = x * 4 + y

    def sizes(p):
        start, length = PARTS[p]
        return start, length // 2, length // 32, start // 2

    def swap(p):
        start, half, piece, hs = sizes(p)
        remote(part_ref.at[at(start + (1 - core) * half, half)], from_core.at[pl.ds(hs, half)],
               sum_send.at[p, 0], sum_recv.at[p, 0], sibling).start()

    def after_swap(p):
        start, half, piece, hs = sizes(p)
        arrived(from_core.at[pl.ds(hs, half)], sum_recv.at[p, 0])
        halves[pl.ds(hs, half), :] = part_ref[at(start + core * half, half), :] + from_core[pl.ds(hs, half), :]
        for d, px, py in plane:
            remote(halves.at[at(hs + (px * 4 + py) * piece, piece)], from_plane.at[d, pl.ds(hs // 16, piece)],
                   sum_send.at[p, 1], sum_recv.at[p, 1], device(core, px, py, z)).start()

    def after_spread(p):
        start, half, piece, hs = sizes(p)
        arrived(from_plane.at[pl.ds(1, 15), pl.ds(hs // 16, piece)], sum_recv.at[p, 1])
        total = halves[at(hs + q * piece, piece), :]
        for d in range(1, 16):
            total = total + from_plane[d, pl.ds(hs // 16, piece), :]
        mine = column.at[z, pl.ds(hs // 16, piece)]
        mine[...] = total
        for d, pz in line:
            remote(mine, mine, sum_send.at[p, 2], sum_recv.at[p, 2], device(core, x, y, pz)).start()

    def after_ring(p):
        start, half, piece, hs = sizes(p)
        arrived(column.at[pl.ds(0, 7), pl.ds(hs // 16, piece)], sum_recv.at[p, 2])
        total = column[0, pl.ds(hs // 16, piece), :]
        for k in range(1, 8):
            total = total + column[k, pl.ds(hs // 16, piece), :]
        mine = sum_ref.at[at(start + core * half + q * piece, piece)]
        mine[...] = total
        for d, px, py in plane:
            remote(mine, mine, sum_send.at[p, 3], sum_recv.at[p, 3], device(core, px, py, z)).start()

    def after_back(p):
        start, half, piece, hs = sizes(p)
        arrived(sum_ref.at[pl.ds(start, 15 * piece)], sum_recv.at[p, 3])

    def last(p):
        start, half, piece, hs = sizes(p)
        mine = sum_ref.at[at(start + core * half, half)]
        remote(mine, mine, sum_send.at[p, 4], sum_recv.at[p, 4], sibling).start()

    def after_last(p):
        start, half, piece, hs = sizes(p)
        arrived(sum_ref.at[pl.ds(start, half)], sum_recv.at[p, 4])

    def all_left(p):
        start, half, piece, hs = sizes(p)
        arrived(from_core.at[pl.ds(hs, half)], sum_send.at[p, 0])
        arrived(from_plane.at[pl.ds(1, 15), pl.ds(hs // 16, piece)], sum_send.at[p, 1])
        arrived(column.at[pl.ds(0, 7), pl.ds(hs // 16, piece)], sum_send.at[p, 2])
        arrived(sum_ref.at[pl.ds(start, 15 * piece)], sum_send.at[p, 3])
        if p == 1:
            arrived(sum_ref.at[pl.ds(start, half)], sum_send.at[p, 4])

    swap(0)
    swap(1)
    after_swap(0)
    after_spread(0)
    diagonal_back()
    after_swap(1)
    after_ring(0)
    after_spread(1)
    diagonal_there()
    after_back(0)

    def between(step):
        @pl.when(step == 0)
        def _():
            after_ring(1)

    cross = sum_ref[at(core * 128, 128), :]
    g_ref[0:128, 0:128] = diag_sum[0:128, :]
    g_ref[0:128, 128:256] = cross
    g_ref[128:256, 0:128] = cross.T
    g_ref[128:256, 128:256] = diag_sum[128:256, :]
    own_factor = level(g_ref, y_ref, between)
    f_ref[core] = own_factor
    mine = f_ref.at[core]
    remote(mine, mine, pair_send.at[0], pair_recv.at[0], sibling).start()
    after_back(1)
    last(1)
    d_ref[core] = left_factor(own_factor, right_factor(g_ref[...], own_factor))
    block = d_ref.at[core]
    remote(block, block, pair_send.at[1], pair_recv.at[1], sibling).start()
    after_last(1)
    between_pairs = jnp.concatenate(
        [jnp.concatenate([sum_ref[256 + 256 * i + 128 * j:384 + 256 * i + 128 * j, :] for j in range(2)], axis=1)
         for i in range(2)], axis=0)
    arrived(f_ref.at[0], pair_recv.at[0])
    f0, f1 = f_ref[0], f_ref[1]
    cross = left_factor(f0, right_factor(between_pairs, f1))
    arrived(d_ref.at[0], pair_recv.at[1])
    g1_ref[0:128, 0:128] = d_ref[0]
    g1_ref[0:128, 128:256] = cross
    g1_ref[128:256, 0:128] = cross.T
    g1_ref[128:256, 128:256] = d_ref[1]
    f = level(g1_ref, y_ref)
    weights = jnp.concatenate([dot(f[0:128], f0, 0, 1, None), dot(f[128:256], f1, 0, 1, None)], axis=1).astype(BF16)
    squares = left_factor(f, right_factor(g1_ref[...], f))
    diagonal = lax.broadcasted_iota(jnp.int32, (128, 128), 0) == lax.broadcasted_iota(jnp.int32, (128, 128), 1)
    squares = jnp.where(diagonal, squares, 0.0)
    inverse = 1.0 / jnp.sqrt(jnp.sum(squares, axis=1, keepdims=True) + EPSILON)
    energies = jnp.sqrt(jnp.sum(squares, axis=0, keepdims=True) + EPSILON)
    share = jnp.zeros((1, 32), F32)
    for j in range(4):
        share = jnp.where(y == j, energies[:, 32 * j:32 * j + 32], share)
    energy_ref[...] = share

    for c in range(CHUNKS):
        block = jnp.concatenate([rows_ref[c, j] for j in range(4)], axis=1)
        part = (dot(weights, block, 1, 1, None) * inverse).astype(BF16)
        for j in range(4):
            sent_ref[c, j] = part[32 * j:32 * j + 32, :]
        for k in (2, 1, 3):
            py = lax.rem(y + k, 4)
            remote(sent_ref.at[c, py], got_ref.at[c, y], out_send, out_recv.at[c], device(core, x, py, z)).start()
    for c in range(CHUNKS):
        basis_ref[:, at(y * R + c * n, n, 128)] = sent_ref[c, y].astype(F32)
    for c in range(CHUNKS):
        arrived(got_ref.at[c, pl.ds(0, 3)], out_recv.at[c])
        for k in (1, 2, 3):
            py = lax.rem(y + k, 4)
            basis_ref[:, at(py * R + c * n, n, 128)] = got_ref[c, py].astype(F32)
    arrived(rows_ref.at[pl.ds(0, 3 * CHUNKS // 4)], row_send)
    diagonal_left()
    for p in range(len(PARTS)):
        all_left(p)
    arrived(f_ref.at[0], pair_send.at[0])
    arrived(d_ref.at[0], pair_send.at[1])
    arrived(got_ref.at[pl.ds(0, 3 * CHUNKS // 4)], out_send)


def body(snapshots):
    R = snapshots.shape[0] // 4
    total = sum(length for _, length in PARTS)
    basis, energies = pl.pallas_call(
        kernel,
        out_shape=(jax.ShapeDtypeStruct((32, 4 * R), F32), jax.ShapeDtypeStruct((1, 32), F32)),
        in_specs=[pl.BlockSpec(memory_space=pl.ANY)],
        out_specs=(pl.BlockSpec(memory_space=pltpu.VMEM),) * 2,
        scratch_shapes=[
            pltpu.VMEM((CHUNKS, 4, R // CHUNKS, 128), BF16),
            pltpu.VMEM((total, 128), F32),
            pltpu.VMEM((total, 128), F32),
            pltpu.VMEM((total // 2, 128), F32),
            pltpu.VMEM((total // 2, 128), F32),
            pltpu.VMEM((16, total // 32, 128), F32),
            pltpu.VMEM((8, total // 32, 128), F32),
            pltpu.VMEM((4 * R, 128), BF16),
            pltpu.VMEM((128, 128), F32),
            pltpu.VMEM((128, 128), F32),
            pltpu.VMEM((4, 32, 128), F32),
            pltpu.VMEM((8, 32, 128), F32),
            pltpu.VMEM((256, 128), F32),
            pltpu.VMEM((256, 256), F32),
            pltpu.VMEM((256, 256), F32),
            pltpu.VMEM((256, 128), F32),
            pltpu.VMEM((2, 256, 128), BF16),
            pltpu.VMEM((2, 128, 128), F32),
            pltpu.VMEM((CHUNKS, 4, 32, R // CHUNKS), BF16),
            pltpu.VMEM((CHUNKS, 4, 32, R // CHUNKS), BF16),
            pltpu.SemaphoreType.DMA,
            pltpu.SemaphoreType.DMA,
            pltpu.SemaphoreType.DMA((4,)),
            pltpu.SemaphoreType.DMA((4,)),
            pltpu.SemaphoreType.DMA,
            pltpu.SemaphoreType.DMA((CHUNKS,)),
            pltpu.SemaphoreType.DMA((2, 5)),
            pltpu.SemaphoreType.DMA((2, 5)),
            pltpu.SemaphoreType.DMA((2,)),
            pltpu.SemaphoreType.DMA((2,)),
            pltpu.SemaphoreType.DMA,
            pltpu.SemaphoreType.DMA((CHUNKS,)),
        ],
        compiler_params=pltpu.CompilerParams(collective_id=0, has_side_effects=True, vmem_limit_bytes=103 * 512 * 1024),
    )(snapshots)
    return basis.T, energies.reshape(32)


def solution(mesh):
    return jax.shard_map(body, mesh=mesh, in_specs=(P("wide", "narrow"),), out_specs=(P("wide", "narrow"), P("narrow")),
                         check_vma=False)
```
